512 devices in a mesh: query: 8 (over y_lo, x), mem: 64 (over z, y_hi, core).
Axes of the slice: x: 4, y: 8 (y_hi: 4, y_lo: 2; y = y_hi * 2 + y_lo), z: 8, core: 2. Of those that a mesh axis runs over, the one named last changes fastest.
Arguments:
- queries: bfloat16 [8, 256, 2560], P('query', 'mem'), may hold values from -6 to 6
- grad_out: bfloat16 [8, 256, 2560], P('query', 'mem'), may hold values from -6 to 6
- attn_out: bfloat16 [8, 256, 2560], P('query', 'mem'), may hold values from -3 to 3
- lse: float32 [8, 256, 20], P('query', 'mem'), may hold values from 2 to 5
- keys: bfloat16 [64, 128, 2560], P('mem'), may hold values from -6 to 6
- values: bfloat16 [64, 128, 2560], P('mem'), may hold values from -6 to 6
- frame_ids: int32 [8, 64], replicated, may hold values from 0 to 63, as said below
- counts: int32 [8], replicated, may hold values from 8 to 64, as said below
Outputs:
- grad_queries: bfloat16 [8, 256, 2560], P('query', 'mem')
- grad_keys: bfloat16 [64, 128, 2560], P('mem', 'query')
- grad_values: bfloat16 [64, 128, 2560], P('mem', 'query')
The draws below stay inside these ranges and needn't reach their ends.
Inputs may be any that keep to these rules, and one draw needn't show every extreme that they name: `frame_ids`: each row lists 64 different memory frames; only the first counts[f] entries of row f count. `counts`: some frame has exactly 64 and some exactly 8.
All inputs are finite; a program needn't handle non-finite values.
Results may differ from the reference program's by a relative error of at most 0.015.
Values may be sent and summed in bfloat16 or wider, within the bound.
No kernel may reach another device: no remote copies, remote signals or barrier semaphores. Data moves between devices by JAX's collectives and lax.ppermute only.
A program may use at most 64 MiB of HBM per device.

```python
import jax
import jax.numpy as jnp
from jax import lax

H = 20
HS = 128
QF = 8
MT = 128
QT = 256
MF = 64
CMAX = 64
N_QUERY = 8


def draw_frame_ids(key, part):
    key = jax.random.fold_in(key, 7)
    jitter = jax.random.randint(key, (QF, MF), 0, MF)
    order_base = jnp.arange(MF, dtype=jnp.int32)
    ranking = (jitter + order_base[None, :]) * MF + order_base[None, :]
    chosen = jnp.argsort(-ranking, axis=1)[:, :CMAX]
    return chosen.astype(jnp.int32)


def draw_counts(key, part):
    key = jax.random.fold_in(key, 8)
    first_key, second_key = jax.random.split(key)
    amounts = jax.random.randint(first_key, (QF,), 8, CMAX + 1)
    shuffled = jax.random.permutation(second_key, QF)
    amounts = amounts.at[shuffled[0]].set(CMAX)
    amounts = amounts.at[shuffled[1]].set(8)
    return amounts.astype(jnp.int32)


def level_of(rng, dims, pieces, least, high):
    factor_of = 1.0
    for dim, blocks in pieces:
        draws = jax.random.uniform(jax.random.fold_in(jax.random.fold_in(rng, 6), dim), (blocks,), jnp.float32, least / len(pieces), high / len(pieces))
        factor_of = factor_of * jnp.repeat(jnp.exp(draws), dims[dim] // blocks).reshape((-1,) + (1,) * (len(dims) - 1 - dim))
    return factor_of


def normal_values(rng, extent, spread, reach, cuts=(), kind=jnp.bfloat16):
    drawn = jax.random.normal(rng, extent, jnp.float32) * spread
    if len(cuts) > 0:
        drawn = level_of(rng, extent, cuts, -0.22, 0.18) * drawn
    return jnp.clip(drawn, min=-reach, max=reach).astype(kind)


def setup_inputs(seed: int = 0) -> dict:
    key_list = jax.random.split(jax.random.key(seed), 9)
    queries = normal_values(key_list[0], (QF, QT, H * HS), 1.0, 6.0, ((0, 8), (1, 64)))
    grad_out = normal_values(key_list[1], (QF, QT, H * HS), 1.0, 6.0, ((0, 8), (1, 64)))
    attn_out = normal_values(key_list[2], (QF, QT, H * HS), 0.5, 3.0, ((0, 8), (1, 64)))
    lse = jnp.clip(2.0 + 3.0 * jax.random.uniform(key_list[3], (QF, QT, H), jnp.float32) ** level_of(key_list[3], (QF, QT, H), ((0, 8), (1, 64)), -0.2, 0.2), 2.0, 5.0)
    keys = normal_values(key_list[4], (MF, MT, H * HS), 1.0, 6.0, ((0, 64),))
    values = normal_values(key_list[5], (MF, MT, H * HS), 1.0, 6.0, ((0, 64),))
    frame_ids = draw_frame_ids(jax.random.fold_in(key_list[8], 71), 0)
    counts = draw_counts(jax.random.fold_in(key_list[8], 71), 0)
    return dict(queries=queries, grad_out=grad_out, attn_out=attn_out, lse=lse, keys=keys, values=values, frame_ids=frame_ids, counts=counts)


def to_low(array):
    return lax.optimization_barrier(array.astype(jnp.bfloat16)).astype(jnp.float32)


def retrieval_mask(frame_ids, counts):
    within = jnp.arange(frame_ids.shape[1], dtype=jnp.int32)[None, :] < counts[:, None]
    frames = jnp.arange(MF, dtype=jnp.int32)
    matches = (frame_ids[:, :, None] == frames[None, None, :]) & within[:, :, None]
    return jnp.where(jnp.any(matches, axis=1), 1.0, 0.0).astype(jnp.float32)


def frame_terms(query_rows, grad_rows, output_rows, lse_rows, key_rows, value_rows, key_mask):
    score_scale = HS ** -0.5
    query_wide = query_rows.astype(jnp.float32)
    grad_wide = grad_rows.astype(jnp.float32)
    row_delta = jnp.sum(grad_wide * output_rows.astype(jnp.float32), axis=-1)
    scores = jnp.einsum('qhd,khd->hqk', query_wide, key_rows) * score_scale
    attn_probs = jnp.exp(scores - jnp.transpose(lse_rows)[:, :, None]) * key_mask[None, None, :]
    probs_low = to_low(attn_probs)
    value_term = jnp.einsum('hqk,qhd->khd', probs_low, grad_wide)
    grad_probs = jnp.einsum('qhd,khd->hqk', grad_wide, value_rows)
    grad_scores = to_low(attn_probs * (grad_probs - jnp.transpose(row_delta)[:, :, None]))
    query_term = jnp.einsum('hqk,khd->qhd', grad_scores, key_rows) * score_scale
    key_term = jnp.einsum('hqk,qhd->khd', grad_scores, query_wide) * score_scale
    return query_term, key_term, value_term


def reference(queries, grad_out, attn_out, lse, keys, values, frame_ids, counts):
    weight_mask = retrieval_mask(frame_ids, counts)
    key_rows = keys.reshape(MF * MT, H, HS).astype(jnp.float32)
    value_rows = values.reshape(MF * MT, H, HS).astype(jnp.float32)
    query_heads = queries.reshape(QF, QT, H, HS)
    grad_heads = grad_out.reshape(QF, QT, H, HS)
    output_heads = attn_out.reshape(QF, QT, H, HS)
    per_group = QF // N_QUERY
    query_grads = []
    total_keys = jnp.zeros((MF * MT, H, HS), jnp.float32)
    total_values = jnp.zeros((MF * MT, H, HS), jnp.float32)
    for group_index in range(N_QUERY):
        part_keys = jnp.zeros((MF * MT, H, HS), jnp.float32)
        part_values = jnp.zeros((MF * MT, H, HS), jnp.float32)
        for member in range(per_group):
            frame_index = group_index * per_group + member
            key_mask = jnp.repeat(weight_mask[frame_index], MT)
            query_term, key_term, value_term = frame_terms(query_heads[frame_index], grad_heads[frame_index], output_heads[frame_index], lse[frame_index], key_rows, value_rows, key_mask)
            query_grads.append(query_term.astype(jnp.bfloat16))
            part_keys = part_keys + key_term
            part_values = part_values + value_term
        total_keys = total_keys + to_low(part_keys)
        total_values = total_values + to_low(part_values)
    grad_queries = jnp.stack(query_grads).reshape(QF, QT, H * HS)
    grad_keys = total_keys.astype(jnp.bfloat16).reshape(MF, MT, H * HS)
    grad_values = total_values.astype(jnp.bfloat16).reshape(MF, MT, H * HS)
    return (grad_queries, grad_keys, grad_values)
```

```python
import functools
import math

import jax
import jax.numpy as jnp
from jax import lax
from jax.experimental import pallas as pl
from jax.experimental.pallas import tpu as pltpu
from jax.sharding import Mesh, PartitionSpec as P

HS = 128
GROUPS = 4
LANES = 128
MASKED = -1e30


def split_low(value):
    high = lax.reduce_precision(value, 8, 7)
    return high.astype(jnp.bfloat16), (value - high).astype(jnp.bfloat16)


def attention_kernel(
    place, amounts, ids, rows, kv_own, kv_core, kv_z, kv_both, dq, own_part, far_part, *, heads
):
    bf16, f32 = jnp.bfloat16, jnp.float32
    score_scale = HS ** (-0.5)
    exponent_scale = score_scale * math.log2(math.e)
    width = heads * HS
    low_frame, low_z = place[0], place[1]
    blocks = (kv_own, kv_core, kv_z, kv_both)
    tokens = kv_own.shape[1]

    frame = lax.broadcasted_iota(jnp.int32, ids.shape, 0)
    entry = lax.broadcasted_iota(jnp.int32, ids.shape, 1)
    limit = jnp.zeros(ids.shape, jnp.int32)
    for f in range(ids.shape[0]):
        limit = jnp.where(frame == f, amounts[f], limit)
    listed = entry < limit
    row8 = lax.broadcasted_iota(jnp.int32, (ids.shape[0], LANES), 0) - low_frame
    lane8 = lax.broadcasted_iota(jnp.int32, (ids.shape[0], LANES), 1)
    spot = (lane8 == 4 * heads + row8) & (row8 >= 0) & (row8 < GROUPS)
    biases = []
    for d in range(4):
        hit = jnp.where((ids[...] == place[2 + d]) & listed, 1.0, 0.0)
        found = jnp.max(hit, axis=1, keepdims=True)
        bias = jnp.sum(jnp.where(spot, (1.0 - found) * MASKED, 0.0), axis=0, keepdims=True)
        biases.append(jnp.broadcast_to(bias, (tokens, LANES)))
    bias_all = jnp.concatenate(biases, axis=0)
    lane = lax.broadcasted_iota(jnp.int32, bias_all.shape, 1)
    extra = rows[:, 2 * width :]

    for h in range(heads):
        cols = slice(h * HS, (h + 1) * HS)
        q = rows[:, cols]
        g = rows[:, width + h * HS : width + (h + 1) * HS]
        k = jnp.concatenate([b[0, :, cols] for b in blocks], axis=0)
        v = jnp.concatenate([b[1, :, cols] for b in blocks], axis=0)
        k_pick = jnp.where((lane == h) | (lane == heads + h), -1.0, bias_all).astype(bf16)
        v_pick = jnp.where((lane == 2 * heads + h) | (lane == 3 * heads + h), -1.0, 0.0).astype(bf16)
        contract = (((1,), (1,)), ((), ()))
        scores = lax.dot_general(
            jnp.concatenate([k, k_pick], axis=1),
            jnp.concatenate([q, extra], axis=1),
            contract,
            preferred_element_type=f32,
        )
        probs = jnp.exp2(scores * exponent_scale)
        grad_probs = lax.dot_general(
            jnp.concatenate([v, v_pick], axis=1),
            jnp.concatenate([g, extra], axis=1),
            contract,
            preferred_element_type=f32,
        )
        grad_scores = (probs * grad_probs).astype(bf16)
        dv = jnp.dot(probs.astype(bf16), g, preferred_element_type=f32).astype(bf16)
        dk = (jnp.dot(grad_scores, q, preferred_element_type=f32) * score_scale).astype(bf16)
        dq_h = lax.dot_general(
            grad_scores, k, (((0,), (0,)), ((), ())), preferred_element_type=f32
        )
        dq[:, cols] = (dq_h * score_scale).astype(bf16)
        for d, out in enumerate((own_part, far_part, own_part, far_part)):
            z = low_z if d < 2 else 1 - low_z
            part = slice(d * tokens, (d + 1) * tokens)
            piece = (out.shape[0], out.shape[3], HS)
            out[:, z, 0, :, cols] = dk[part].reshape(piece)
            out[:, z, 1, :, cols] = dv[part].reshape(piece)


def on_device(sizes, queries, grad_out, attn_out, lse, keys, values, frame_ids, counts):
    f32, bf16 = jnp.float32, jnp.bfloat16
    low_y, x = lax.axis_index("yl"), lax.axis_index("x")
    high_z, low_z = lax.axis_index("zh"), lax.axis_index("zl")
    high_y, core = lax.axis_index("yh"), lax.axis_index("c")
    tokens_here, columns = queries.shape[1], queries.shape[2]
    heads = lse.shape[2] // GROUPS
    width = heads * HS
    frame_tokens = keys.shape[1]
    spread = sizes["zh"] * sizes["yh"]
    members = GROUPS * spread
    blocks_q = sizes["yl"] * sizes["x"]

    kv = jnp.stack(
        [lax.dynamic_slice_in_dim(a[0], x * width, width, 1) for a in (keys, values)]
    )
    flip = [(0, 1), (1, 0)]
    both = [(a * 2 + b, (1 - a) * 2 + (1 - b)) for a in range(2) for b in range(2)]
    kv_core = lax.ppermute(kv, "c", flip)
    kv_z = lax.ppermute(kv, "zl", flip)
    kv_both = lax.ppermute(kv, ("zl", "c"), both)

    delta = jnp.sum(
        (grad_out[0].astype(f32) * attn_out[0].astype(f32)).reshape(tokens_here, -1, HS), axis=-1
    )
    lse_high, lse_low = split_low(lse[0] * HS**0.5)
    delta_high, delta_low = split_low(delta)
    by_group = lambda a: a.reshape(tokens_here, GROUPS, -1).transpose(1, 0, 2)
    frame_spot = (jnp.arange(LANES - 4 * heads) == x).astype(bf16)
    packed = jnp.concatenate(
        [
            by_group(queries[0]),
            by_group(grad_out[0]),
            by_group(lse_high),
            by_group(lse_low),
            by_group(delta_high),
            by_group(delta_low),
            jnp.broadcast_to(frame_spot, (GROUPS, tokens_here, LANES - 4 * heads)),
        ],
        axis=2,
    )
    packed = jnp.broadcast_to(
        packed[:, None], (GROUPS, spread, tokens_here, packed.shape[2])
    ).reshape(members, tokens_here, -1)
    rows = lax.all_to_all(packed, ("x", "zh", "yh"), 0, 0, tiled=True)
    rows = rows.reshape(members * tokens_here, -1)

    def memory_frame(z, c):
        return ((high_z * 2 + z) * sizes["yh"] + high_y) * 2 + c

    place = jnp.stack(
        [
            low_y * GROUPS,
            low_z,
            memory_frame(low_z, core),
            memory_frame(low_z, 1 - core),
            memory_frame(1 - low_z, core),
            memory_frame(1 - low_z, 1 - core),
        ]
    ).astype(jnp.int32)
    in_vmem = pl.BlockSpec(memory_space=pltpu.VMEM)
    in_smem = pl.BlockSpec(memory_space=pltpu.SMEM)
    part = jax.ShapeDtypeStruct((blocks_q, 2, 2, frame_tokens // blocks_q, width), bf16)
    dq, own_part, far_part = pl.pallas_call(
        functools.partial(attention_kernel, heads=heads),
        out_shape=(jax.ShapeDtypeStruct((rows.shape[0], width), bf16), part, part),
        in_specs=[in_smem, in_smem] + [in_vmem] * 6,
        out_specs=(in_vmem,) * 3,
        compiler_params=pltpu.CompilerParams(vmem_limit_bytes=40 * 2**20),
        name="attention_grads",
    )(place, counts, frame_ids, rows, kv, kv_core, kv_z, kv_both)

    far_part = lax.ppermute(far_part, "c", flip)

    dq = lax.all_to_all(
        dq.reshape(members, tokens_here, width), ("x", "zh", "yh"), 0, 0, tiled=True
    )
    dq = jnp.sum(dq.reshape(GROUPS, spread, tokens_here, width).astype(f32), axis=1)
    grad_queries = dq.transpose(1, 0, 2).reshape(1, tokens_here, columns).astype(bf16)

    pair = (own_part.astype(f32) + far_part.astype(f32)).astype(bf16)
    pair = pair.reshape(blocks_q * 2, 2, frame_tokens // blocks_q, width)
    pair = lax.all_to_all(pair, ("yl", "x", "zl"), 0, 0, tiled=True)
    pair = pair.reshape(sizes["yl"], GROUPS, 2, 2, frame_tokens // blocks_q, width)
    total = jnp.sum(pair.astype(f32), axis=(0, 2))
    total = total.transpose(1, 2, 0, 3).reshape(2, 1, frame_tokens // blocks_q, columns)
    total = total.astype(bf16)
    return grad_queries, total[0], total[1]


def solution(mesh):
    query, mem = mesh.shape["query"], mesh.shape["mem"]
    sizes = {"yl": query // GROUPS, "x": GROUPS, "zh": mem // 16, "zl": 2, "yh": 4, "c": 2}
    if mem < 16:
        sizes.update(zh=1, yh=mem // 4)
    fine = Mesh(mesh.devices.reshape(tuple(sizes.values())), tuple(sizes))
    q_axes, m_axes = ("yl", "x"), ("zh", "zl", "yh", "c")
    rows = P(q_axes, m_axes, None)
    frames = P(m_axes, None, None)
    return jax.shard_map(
        functools.partial(on_device, sizes),
        mesh=fine,
        in_specs=(rows, rows, rows, rows, frames, frames, P(), P()),
        out_specs=(rows, P(m_axes, q_axes, None), P(m_axes, q_axes, None)),
        check_vma=False,
    )
```

```python
import functools
import math

import jax
import jax.numpy as jnp
from jax import lax
from jax.experimental import pallas as pl
from jax.experimental.pallas import tpu as pltpu
from jax.sharding import Mesh, PartitionSpec as P

HS = 128
GROUPS = 4
LANES = 128
MASKED = -1e30
F32, BF16 = jnp.float32, jnp.bfloat16
IN_VMEM = pl.BlockSpec(memory_space=pltpu.VMEM)
IN_SMEM = pl.BlockSpec(memory_space=pltpu.SMEM)


def call(body, name, out_shape, in_specs, *args):
    return pl.pallas_call(
        body,
        out_shape=out_shape,
        in_specs=in_specs,
        out_specs=jax.tree.map(lambda _: IN_VMEM, out_shape),
        compiler_params=pltpu.CompilerParams(vmem_limit_bytes=40 * 2**20),
        name=name,
    )(*args)


def pack_rows(place, queries, grad_out, attn_out, lse, out, *, heads):
    width = heads * HS
    tokens = queries.shape[1]
    lane = lax.broadcasted_iota(jnp.int32, (tokens, LANES), 1)
    lse_scaled = lse[0] * HS**0.5
    for group in range(GROUPS):
        extra = jnp.where(lane == 4 * heads + place[0], 1.0, 0.0).astype(F32)
        for h in range(heads):
            head = group * heads + h
            cols = slice(head * HS, (head + 1) * HS)
            product = grad_out[0, :, cols].astype(F32) * attn_out[0, :, cols].astype(F32)
            delta = jnp.sum(product, axis=1, keepdims=True)
            for i, value in enumerate((lse_scaled[:, head : head + 1], delta)):
                high = value.astype(BF16).astype(F32)
                extra = jnp.where(lane == 2 * i * heads + h, high, extra)
                extra = jnp.where(lane == (2 * i + 1) * heads + h, value - high, extra)
        cols = slice(group * width, (group + 1) * width)
        row = jnp.concatenate(
            [queries[0, :, cols], grad_out[0, :, cols], extra.astype(BF16)], axis=1
        )
        for s in range(out.shape[0] // GROUPS):
            out[s * GROUPS + group] = row


def attention_grads(
    place, amounts, ids, rows, kv_own, kv_core, kv_z, kv_both, dq, near, far, *, heads
):
    score_scale = HS ** (-0.5)
    exponent_scale = score_scale * math.log2(math.e)
    width = heads * HS
    blocks = (kv_own, kv_core, kv_z, kv_both)
    tokens = kv_own.shape[1]

    frame = lax.broadcasted_iota(jnp.int32, ids.shape, 0)
    entry = lax.broadcasted_iota(jnp.int32, ids.shape, 1)
    limit = jnp.zeros(ids.shape, jnp.int32)
    for f in range(ids.shape[0]):
        limit = jnp.where(frame == f, amounts[f], limit)
    listed = entry < limit
    row8 = lax.broadcasted_iota(jnp.int32, (ids.shape[0], LANES), 0) - place[1] * GROUPS
    lane8 = lax.broadcasted_iota(jnp.int32, (ids.shape[0], LANES), 1)
    spot = (lane8 == 4 * heads + row8) & (row8 >= 0) & (row8 < GROUPS)
    biases = []
    for d in range(4):
        hit = jnp.where((ids[...] == place[2 + d]) & listed, 1.0, 0.0)
        found = jnp.max(hit, axis=1, keepdims=True)
        bias = jnp.sum(jnp.where(spot, (1.0 - found) * MASKED, 0.0), axis=0, keepdims=True)
        biases.append(jnp.broadcast_to(bias, (tokens, LANES)))
    bias_all = jnp.concatenate(biases, axis=0)
    lane = lax.broadcasted_iota(jnp.int32, bias_all.shape, 1)
    extra = rows[:, 2 * width :]

    for h in range(heads):
        cols = slice(h * HS, (h + 1) * HS)
        q = rows[:, cols]
        g = rows[:, width + h * HS : width + (h + 1) * HS]
        k = jnp.concatenate([b[0, :, cols] for b in blocks], axis=0)
        v = jnp.concatenate([b[1, :, cols] for b in blocks], axis=0)
        k_pick = jnp.where((lane == h) | (lane == heads + h), -1.0, bias_all).astype(BF16)
        v_pick = jnp.where((lane == 2 * heads + h) | (lane == 3 * heads + h), -1.0, 0.0).astype(BF16)
        contract = (((1,), (1,)), ((), ()))
        scores = lax.dot_general(
            jnp.concatenate([k, k_pick], axis=1),
            jnp.concatenate([q, extra], axis=1),
            contract,
            preferred_element_type=F32,
        )
        probs = jnp.exp2(scores * exponent_scale)
        grad_probs = lax.dot_general(
            jnp.concatenate([v, v_pick], axis=1),
            jnp.concatenate([g, extra], axis=1),
            contract,
            preferred_element_type=F32,
        )
        grad_scores = (probs * grad_probs).astype(BF16)
        dv = jnp.dot(probs.astype(BF16), g, preferred_element_type=F32).astype(BF16)
        dk = (jnp.dot(grad_scores, q, preferred_element_type=F32) * score_scale).astype(BF16)
        dq_h = lax.dot_general(
            grad_scores, k, (((0,), (0,)), ((), ())), preferred_element_type=F32
        )
        dq[:, cols] = (dq_h * score_scale).astype(BF16)
        for d, out in enumerate((near, far, near, far)):
            part = slice(d * tokens, (d + 1) * tokens)
            piece = (out.shape[1], out.shape[3], HS)
            out[d // 2, :, 0, :, cols] = dk[part].reshape(piece)
            out[d // 2, :, 1, :, cols] = dv[part].reshape(piece)


def pack_terms(dq, near, from_core, from_z, out):
    share = near.shape[3]
    dq_sum = dq[0].astype(F32)
    for s in range(1, dq.shape[0]):
        dq_sum = dq_sum + dq[s].astype(F32)
    tokens = dq.shape[1] // GROUPS
    for b in range(out.shape[0]):
        for kind in range(2):
            total = near[0, b, kind].astype(F32) + from_core[0, b, kind].astype(F32)
            total = total + from_z[b, kind].astype(F32)
            out[b, kind * share : (kind + 1) * share] = total.astype(BF16)
        x = b % GROUPS
        piece = dq_sum[x * tokens : (x + 1) * tokens]
        rest = jnp.zeros((out.shape[1] - 2 * share - tokens, piece.shape[1]), F32)
        out[b, 2 * share :] = jnp.concatenate([piece, rest], axis=0).astype(BF16)


def unpack_terms(place, terms, grad_queries, grad_keys, grad_values):
    share, tokens = grad_keys.shape[1], grad_queries.shape[1]
    width = terms.shape[2]
    for x in range(GROUPS):
        cols = slice(x * width, (x + 1) * width)
        for kind, out in enumerate((grad_keys, grad_values)):
            part = slice(kind * share, (kind + 1) * share)
            total = terms[x, part].astype(F32)
            for y in range(1, terms.shape[0] // GROUPS):
                total = total + terms[y * GROUPS + x, part].astype(F32)
            out[0, :, cols] = total.astype(BF16)
        mine = terms[place[1] * GROUPS + x, 2 * share :].astype(F32)
        grad_queries[0, :, cols] = mine[:tokens].astype(BF16)


def on_device(sizes, queries, grad_out, attn_out, lse, keys, values, frame_ids, counts):
    low_y, x = lax.axis_index("yl"), lax.axis_index("x")
    high_z, low_z = lax.axis_index("zh"), lax.axis_index("zl")
    high_y, core = lax.axis_index("yh"), lax.axis_index("c")
    tokens_here = queries.shape[1]
    heads = lse.shape[2] // GROUPS
    width = heads * HS
    frame_tokens = keys.shape[1]
    spread = sizes["zh"] * sizes["yh"]
    members = GROUPS * spread
    blocks_q = sizes["yl"] * sizes["x"]
    share = frame_tokens // blocks_q

    def memory_frame(z, c):
        return ((high_z * 2 + z) * sizes["yh"] + high_y) * 2 + c

    place = jnp.stack(
        [
            x,
            low_y,
            memory_frame(low_z, core),
            memory_frame(low_z, 1 - core),
            memory_frame(1 - low_z, core),
            memory_frame(1 - low_z, 1 - core),
        ]
    ).astype(jnp.int32)

    packed = call(
        functools.partial(pack_rows, heads=heads),
        "pack_rows",
        jax.ShapeDtypeStruct((members, tokens_here, 2 * width + LANES), BF16),
        [IN_SMEM] + [IN_VMEM] * 4,
        place,
        queries,
        grad_out,
        attn_out,
        lse,
    )
    rows = lax.all_to_all(packed, ("zh", "yh", "x"), 0, 0, tiled=True)
    rows = rows.reshape(members * tokens_here, -1)

    kv = jnp.stack(
        [lax.dynamic_slice_in_dim(a[0], x * width, width, 1) for a in (keys, values)]
    )
    flip = [(0, 1), (1, 0)]
    kv_z = lax.ppermute(kv, "zl", flip)
    kv_core = lax.ppermute(kv, "c", flip)
    kv_both = lax.ppermute(kv_z, "c", flip)

    part = jax.ShapeDtypeStruct((2, blocks_q, 2, share, width), BF16)
    dq, near, far = call(
        functools.partial(attention_grads, heads=heads),
        "attention_grads",
        (jax.ShapeDtypeStruct((rows.shape[0], width), BF16), part, part),
        [IN_SMEM] * 2 + [IN_VMEM] * 6,
        place,
        counts,
        frame_ids,
        rows,
        kv,
        kv_core,
        kv_z,
        kv_both,
    )

    from_core = lax.ppermute(far, "c", flip)
    dq = lax.all_to_all(
        dq.reshape(spread, GROUPS * tokens_here, width), ("zh", "yh"), 0, 0, tiled=True
    )
    other_z = (near[1].astype(F32) + from_core[1].astype(F32)).astype(BF16)
    from_z = lax.ppermute(other_z, "zl", flip)
    terms = call(
        pack_terms,
        "pack_terms",
        jax.ShapeDtypeStruct((blocks_q, 2 * share + 2 * tokens_here, width), BF16),
        [IN_VMEM] * 4,
        dq,
        near,
        from_core,
        from_z,
    )
    terms = lax.all_to_all(terms, ("yl", "x"), 0, 0, tiled=True)
    return call(
        unpack_terms,
        "unpack_terms",
        (
            jax.ShapeDtypeStruct(queries.shape, BF16),
            jax.ShapeDtypeStruct((1, share, keys.shape[2]), BF16),
            jax.ShapeDtypeStruct((1, share, keys.shape[2]), BF16),
        ),
        [IN_SMEM, IN_VMEM],
        place,
        terms,
    )


def solution(mesh):
    query, mem = mesh.shape["query"], mesh.shape["mem"]
    sizes = {"yl": query // GROUPS, "x": GROUPS, "zh": mem // 16, "zl": 2, "yh": 4, "c": 2}
    if mem < 16:
        sizes.update(zh=1, yh=mem // 4)
    fine = Mesh(mesh.devices.reshape(tuple(sizes.values())), tuple(sizes))
    q_axes, m_axes = ("yl", "x"), ("zh", "zl", "yh", "c")
    rows = P(q_axes, m_axes, None)
    frames = P(m_axes, None, None)
    return jax.shard_map(
        functools.partial(on_device, sizes),
        mesh=fine,
        in_specs=(rows, rows, rows, rows, frames, frames, P(), P()),
        out_specs=(rows, P(m_axes, q_axes, None), P(m_axes, q_axes, None)),
        check_vma=False,
    )
```

```python
import functools
import math

import jax
import jax.numpy as jnp
from jax import lax
from jax.experimental import pallas as pl
from jax.experimental.pallas import tpu as pltpu
from jax.sharding import Mesh, PartitionSpec as P

HS = 128
GROUPS = 4
LANES = 128
MASKED = -1e30
F32, BF16 = jnp.float32, jnp.bfloat16
IN_VMEM = pl.BlockSpec(memory_space=pltpu.VMEM)
IN_SMEM = pl.BlockSpec(memory_space=pltpu.SMEM)
IN_PLACE = pl.BlockSpec(memory_space=pl.ANY)


LONG = pl.CostEstimate(flops=10**11, bytes_accessed=10**6, transcendentals=0)


def call(body, name, out_shape, in_specs, *args, cost=None, scratch=(), vmem=40):
    return pl.pallas_call(
        body,
        out_shape=out_shape,
        in_specs=in_specs,
        scratch_shapes=scratch,
        cost_estimate=cost,
        out_specs=jax.tree.map(lambda _: IN_VMEM, out_shape),
        compiler_params=pltpu.CompilerParams(vmem_limit_bytes=vmem * 2**20),
        name=name,
    )(*args)


def pack_rows(
    place, queries, grad_out, attn_out, lse, keys, values, out, kv, key_copied, value_copied, *, heads
):
    width = heads * HS
    here = pl.ds(pl.multiple_of(place[0] * width, LANES), width)
    copies = [
        pltpu.make_async_copy(keys.at[0, :, here], kv.at[0], key_copied),
        pltpu.make_async_copy(values.at[0, :, here], kv.at[1], value_copied),
    ]
    for copy in copies:
        copy.start()
    tokens = queries.shape[1]
    lane = lax.broadcasted_iota(jnp.int32, (tokens, LANES), 1)
    lse_scaled = lse[0] * HS**0.5
    for group in range(GROUPS):
        extra = jnp.where(lane == 4 * heads + place[0], 1.0, 0.0).astype(F32)
        for h in range(heads):
            head = group * heads + h
            cols = slice(head * HS, (head + 1) * HS)
            product = grad_out[0, :, cols].astype(F32) * attn_out[0, :, cols].astype(F32)
            delta = jnp.sum(product, axis=1, keepdims=True)
            for i, value in enumerate((lse_scaled[:, head : head + 1], delta)):
                high = value.astype(BF16).astype(F32)
                extra = jnp.where(lane == 2 * i * heads + h, high, extra)
                extra = jnp.where(lane == (2 * i + 1) * heads + h, value - high, extra)
        cols = slice(group * width, (group + 1) * width)
        row = jnp.concatenate(
            [queries[0, :, cols], grad_out[0, :, cols], extra.astype(BF16)], axis=1
        )
        for s in range(out.shape[0] // GROUPS):
            out[s * GROUPS + group] = row
    for copy in copies:
        copy.wait()


def pair_frames(kv_own, kv_z, out):
    out[0] = kv_own[...]
    out[1] = kv_z[...]


def attention_grads(
    place, amounts, ids, rows, kv_own, kv_core, dq, near, far, *, heads
):
    score_scale = HS ** (-0.5)
    exponent_scale = score_scale * math.log2(math.e)
    width = heads * HS
    blocks = (kv_own.at[0], kv_core.at[0], kv_own.at[1], kv_core.at[1])
    tokens = kv_own.shape[2]

    frame = lax.broadcasted_iota(jnp.int32, ids.shape, 0)
    entry = lax.broadcasted_iota(jnp.int32, ids.shape, 1)
    limit = jnp.zeros(ids.shape, jnp.int32)
    for f in range(ids.shape[0]):
        limit = jnp.where(frame == f, amounts[f], limit)
    listed = entry < limit
    row8 = lax.broadcasted_iota(jnp.int32, (ids.shape[0], LANES), 0) - place[1] * GROUPS
    lane8 = lax.broadcasted_iota(jnp.int32, (ids.shape[0], LANES), 1)
    spot = (lane8 == 4 * heads + row8) & (row8 >= 0) & (row8 < GROUPS)
    biases = []
    for d in range(4):
        hit = jnp.where((ids[...] == place[2 + d]) & listed, 1.0, 0.0)
        found = jnp.max(hit, axis=1, keepdims=True)
        bias = jnp.sum(jnp.where(spot, (1.0 - found) * MASKED, 0.0), axis=0, keepdims=True)
        biases.append(jnp.broadcast_to(bias, (tokens, LANES)))
    bias_all = jnp.concatenate(biases, axis=0)
    lane = lax.broadcasted_iota(jnp.int32, bias_all.shape, 1)
    extra = rows[:, 2 * width :]

    for h in range(heads):
        cols = slice(h * HS, (h + 1) * HS)
        q = rows[:, cols]
        g = rows[:, width + h * HS : width + (h + 1) * HS]
        k = jnp.concatenate([b[0, :, cols] for b in blocks], axis=0)
        v = jnp.concatenate([b[1, :, cols] for b in blocks], axis=0)
        k_pick = jnp.where((lane == h) | (lane == heads + h), -1.0, bias_all).astype(BF16)
        v_pick = jnp.where((lane == 2 * heads + h) | (lane == 3 * heads + h), -1.0, 0.0).astype(BF16)
        contract = (((1,), (1,)), ((), ()))
        scores = lax.dot_general(
            jnp.concatenate([k, k_pick], axis=1),
            jnp.concatenate([q, extra], axis=1),
            contract,
            preferred_element_type=F32,
        )
        probs = jnp.exp2(scores * exponent_scale)
        grad_probs = lax.dot_general(
            jnp.concatenate([v, v_pick], axis=1),
            jnp.concatenate([g, extra], axis=1),
            contract,
            preferred_element_type=F32,
        )
        grad_scores = (probs * grad_probs).astype(BF16)
        dv = jnp.dot(probs.astype(BF16), g, preferred_element_type=F32).astype(BF16)
        dk = (jnp.dot(grad_scores, q, preferred_element_type=F32) * score_scale).astype(BF16)
        dq_h = lax.dot_general(
            grad_scores, k, (((0,), (0,)), ((), ())), preferred_element_type=F32
        )
        dq[:, cols] = (dq_h * score_scale).astype(BF16)
        for d, out in enumerate((near, far, near, far)):
            part = slice(d * tokens, (d + 1) * tokens)
            piece = (out.shape[1], out.shape[3], HS)
            out[d // 2, :, 0, :, cols] = dk[part].reshape(piece)
            out[d // 2, :, 1, :, cols] = dv[part].reshape(piece)


def add_core(near, from_core, out):
    out[...] = (near[1].astype(F32) + from_core[1].astype(F32)).astype(BF16)


def add_z(near, from_core, from_z, out):
    total = near[0].astype(F32) + from_core[0].astype(F32)
    out[...] = (total + from_z[...].astype(F32)).astype(BF16)


def pack_terms(dq, part, out):
    share = part.shape[2]
    dq_sum = dq[0].astype(F32)
    for s in range(1, dq.shape[0]):
        dq_sum = dq_sum + dq[s].astype(F32)
    tokens = dq.shape[1] // GROUPS
    for b in range(out.shape[0]):
        for kind in range(2):
            out[b, kind * share : (kind + 1) * share] = part[b, kind]
        x = b % GROUPS
        piece = dq_sum[x * tokens : (x + 1) * tokens]
        rest = jnp.zeros((out.shape[1] - 2 * share - tokens, piece.shape[1]), F32)
        out[b, 2 * share :] = jnp.concatenate([piece, rest], axis=0).astype(BF16)


def unpack_terms(place, terms, grad_queries, grad_keys, grad_values):
    share, tokens = grad_keys.shape[1], grad_queries.shape[1]
    width = terms.shape[2]
    for x in range(GROUPS):
        cols = slice(x * width, (x + 1) * width)
        for kind, out in enumerate((grad_keys, grad_values)):
            part = slice(kind * share, (kind + 1) * share)
            total = terms[x, part].astype(F32)
            for y in range(1, terms.shape[0] // GROUPS):
                total = total + terms[y * GROUPS + x, part].astype(F32)
            out[0, :, cols] = total.astype(BF16)
        mine = terms[place[1] * GROUPS + x, 2 * share :].astype(F32)
        grad_queries[0, :, cols] = mine[:tokens].astype(BF16)


def on_device(sizes, queries, grad_out, attn_out, lse, keys, values, frame_ids, counts):
    low_y, x = lax.axis_index("yl"), lax.axis_index("x")
    high_z, low_z = lax.axis_index("zh"), lax.axis_index("zl")
    high_y, core = lax.axis_index("yh"), lax.axis_index("c")
    tokens_here = queries.shape[1]
    heads = lse.shape[2] // GROUPS
    width = heads * HS
    frame_tokens = keys.shape[1]
    spread = sizes["zh"] * sizes["yh"]
    members = GROUPS * spread
    blocks_q = sizes["yl"] * sizes["x"]
    share = frame_tokens // blocks_q

    def memory_frame(z, c):
        return ((high_z * 2 + z) * sizes["yh"] + high_y) * 2 + c

    place = jnp.stack(
        [
            x,
            low_y,
            memory_frame(low_z, core),
            memory_frame(low_z, 1 - core),
            memory_frame(1 - low_z, core),
            memory_frame(1 - low_z, 1 - core),
        ]
    ).astype(jnp.int32)

    flip = [(0, 1), (1, 0)]
    packed, kv = call(
        functools.partial(pack_rows, heads=heads),
        "pack_rows",
        (
            jax.ShapeDtypeStruct((members, tokens_here, 2 * width + LANES), BF16),
            jax.ShapeDtypeStruct((2, frame_tokens, width), BF16),
        ),
        [IN_SMEM] + [IN_VMEM] * 4 + [IN_PLACE] * 2,
        place,
        queries,
        grad_out,
        attn_out,
        lse,
        keys,
        values,
        scratch=[pltpu.SemaphoreType.DMA] * 2,
        vmem=60,
    )
    rows = lax.all_to_all(packed, ("zh", "yh", "x"), 0, 0, tiled=True)
    rows = rows.reshape(members * tokens_here, -1)

    kv_z = lax.ppermute(kv, "zl", flip)
    kv_own = call(
        pair_frames,
        "pair_frames",
        jax.ShapeDtypeStruct((2,) + kv.shape, BF16),
        [IN_VMEM] * 2,
        kv,
        kv_z,
        cost=LONG,
    )
    kv_core = lax.ppermute(kv_own, "c", flip)

    part = jax.ShapeDtypeStruct((2, blocks_q, 2, share, width), BF16)
    half = jax.ShapeDtypeStruct(part.shape[1:], BF16)
    dq, near, far = call(
        functools.partial(attention_grads, heads=heads),
        "attention_grads",
        (jax.ShapeDtypeStruct((rows.shape[0], width), BF16), part, part),
        [IN_SMEM] * 2 + [IN_VMEM] * 4,
        place,
        counts,
        frame_ids,
        rows,
        kv_own,
        kv_core,
    )

    from_core = lax.ppermute(far, "c", flip)
    other_z = call(add_core, "add_core", half, [IN_VMEM] * 2, near, from_core)
    from_z = lax.ppermute(other_z, "zl", flip)
    mine = call(
        add_z, "add_z", half, [IN_VMEM] * 3, near, from_core, from_z, cost=LONG
    )
    dq = lax.all_to_all(
        dq.reshape(spread, GROUPS * tokens_here, width), ("zh", "yh"), 0, 0, tiled=True
    )
    terms = call(
        pack_terms,
        "pack_terms",
        jax.ShapeDtypeStruct((blocks_q, 2 * share + 2 * tokens_here, width), BF16),
        [IN_VMEM] * 2,
        dq,
        mine,
    )
    terms = lax.all_to_all(terms, ("yl", "x"), 0, 0, tiled=True)
    return call(
        unpack_terms,
        "unpack_terms",
        (
            jax.ShapeDtypeStruct(queries.shape, BF16),
            jax.ShapeDtypeStruct((1, share, keys.shape[2]), BF16),
            jax.ShapeDtypeStruct((1, share, keys.shape[2]), BF16),
        ),
        [IN_SMEM, IN_VMEM],
        place,
        terms,
    )


def solution(mesh):
    query, mem = mesh.shape["query"], mesh.shape["mem"]
    sizes = {"yl": query // GROUPS, "x": GROUPS, "zh": mem // 16, "zl": 2, "yh": 4, "c": 2}
    if mem < 16:
        sizes.update(zh=1, yh=mem // 4)
    fine = Mesh(mesh.devices.reshape(tuple(sizes.values())), tuple(sizes))
    q_axes, m_axes = ("yl", "x"), ("zh", "zl", "yh", "c")
    rows = P(q_axes, m_axes, None)
    frames = P(m_axes, None, None)
    return jax.shard_map(
        functools.partial(on_device, sizes),
        mesh=fine,
        in_specs=(rows, rows, rows, rows, frames, frames, P(), P()),
        out_specs=(rows, P(m_axes, q_axes, None), P(m_axes, q_axes, None)),
        check_vma=False,
    )
```

```python
import functools
import math

import jax
import jax.numpy as jnp
from jax import lax
from jax.experimental import pallas as pl
from jax.experimental.pallas import tpu as pltpu
from jax.sharding import Mesh, PartitionSpec as P

HS = 128
GROUPS = 4
LANES = 128
MASKED = -1e30
F32, BF16 = jnp.float32, jnp.bfloat16
IN_VMEM = pl.BlockSpec(memory_space=pltpu.VMEM)
IN_SMEM = pl.BlockSpec(memory_space=pltpu.SMEM)


def call(body, name, out_shape, in_specs, *args):
    return pl.pallas_call(
        body,
        out_shape=out_shape,
        in_specs=in_specs,
        out_specs=jax.tree.map(lambda _: IN_VMEM, out_shape),
        compiler_params=pltpu.CompilerParams(vmem_limit_bytes=40 * 2**20),
        name=name,
    )(*args)


def pack_rows(place, queries, grad_out, attn_out, lse, out, *, heads):
    width = heads * HS
    tokens = queries.shape[1]
    lane = lax.broadcasted_iota(jnp.int32, (tokens, LANES), 1)
    lse_scaled = lse[0] * HS**0.5
    for group in range(GROUPS):
        extra = jnp.where(lane == 4 * heads + place[0], 1.0, 0.0).astype(F32)
        for h in range(heads):
            head = group * heads + h
            cols = slice(head * HS, (head + 1) * HS)
            product = grad_out[0, :, cols].astype(F32) * attn_out[0, :, cols].astype(F32)
            delta = jnp.sum(product, axis=1, keepdims=True)
            for i, value in enumerate((lse_scaled[:, head : head + 1], delta)):
                high = value.astype(BF16).astype(F32)
                extra = jnp.where(lane == 2 * i * heads + h, high, extra)
                extra = jnp.where(lane == (2 * i + 1) * heads + h, value - high, extra)
        cols = slice(group * width, (group + 1) * width)
        row = jnp.concatenate(
            [queries[0, :, cols], grad_out[0, :, cols], extra.astype(BF16)], axis=1
        )
        for s in range(out.shape[0] // GROUPS):
            out[s * GROUPS + group] = row


def attention_grads(
    place, amounts, ids, rows, kv, dq, near, far, *, heads
):
    score_scale = HS ** (-0.5)
    exponent_scale = score_scale * math.log2(math.e)
    width = heads * HS
    blocks = [kv.at[place[7 + d]] for d in range(4)]
    tokens = kv.shape[2]

    frame = lax.broadcasted_iota(jnp.int32, ids.shape, 0)
    entry = lax.broadcasted_iota(jnp.int32, ids.shape, 1)
    limit = jnp.zeros(ids.shape, jnp.int32)
    for f in range(ids.shape[0]):
        limit = jnp.where(frame == f, amounts[f], limit)
    listed = entry < limit
    row8 = lax.broadcasted_iota(jnp.int32, (ids.shape[0], LANES), 0) - place[1] * GROUPS
    lane8 = lax.broadcasted_iota(jnp.int32, (ids.shape[0], LANES), 1)
    spot = (lane8 == 4 * heads + row8) & (row8 >= 0) & (row8 < GROUPS)
    biases = []
    for d in range(4):
        hit = jnp.where((ids[...] == place[3 + d]) & listed, 1.0, 0.0)
        found = jnp.max(hit, axis=1, keepdims=True)
        bias = jnp.sum(jnp.where(spot, (1.0 - found) * MASKED, 0.0), axis=0, keepdims=True)
        biases.append(jnp.broadcast_to(bias, (tokens, LANES)))
    bias_all = jnp.concatenate(biases, axis=0)
    lane = lax.broadcasted_iota(jnp.int32, bias_all.shape, 1)
    extra = rows[:, 2 * width :]

    for h in range(heads):
        cols = slice(h * HS, (h + 1) * HS)
        q = rows[:, cols]
        g = rows[:, width + h * HS : width + (h + 1) * HS]
        k = jnp.concatenate([b[0, :, cols] for b in blocks], axis=0)
        v = jnp.concatenate([b[1, :, cols] for b in blocks], axis=0)
        k_pick = jnp.where((lane == h) | (lane == heads + h), -1.0, bias_all).astype(BF16)
        v_pick = jnp.where((lane == 2 * heads + h) | (lane == 3 * heads + h), -1.0, 0.0).astype(BF16)
        contract = (((1,), (1,)), ((), ()))
        scores = lax.dot_general(
            jnp.concatenate([k, k_pick], axis=1),
            jnp.concatenate([q, extra], axis=1),
            contract,
            preferred_element_type=F32,
        )
        probs = jnp.exp2(scores * exponent_scale)
        grad_probs = lax.dot_general(
            jnp.concatenate([v, v_pick], axis=1),
            jnp.concatenate([g, extra], axis=1),
            contract,
            preferred_element_type=F32,
        )
        grad_scores = (probs * grad_probs).astype(BF16)
        dv = jnp.dot(probs.astype(BF16), g, preferred_element_type=F32).astype(BF16)
        dk = (jnp.dot(grad_scores, q, preferred_element_type=F32) * score_scale).astype(BF16)
        dq_h = lax.dot_general(
            grad_scores, k, (((0,), (0,)), ((), ())), preferred_element_type=F32
        )
        dq[:, cols] = (dq_h * score_scale).astype(BF16)
        for d, out in enumerate((near, far, near, far)):
            part = slice(d * tokens, (d + 1) * tokens)
            z = place[2] if d < 2 else 1 - place[2]
            piece = (out.shape[0], out.shape[3], HS)
            out[:, z, 0, :, cols] = dk[part].reshape(piece)
            out[:, z, 1, :, cols] = dv[part].reshape(piece)


def pack_terms(dq, near, from_core, out):
    share = near.shape[3]
    dq_sum = dq[0].astype(F32)
    for s in range(1, dq.shape[0]):
        dq_sum = dq_sum + dq[s].astype(F32)
    tokens = dq.shape[1] // GROUPS
    rest = jnp.zeros((out.shape[1] - 2 * share - tokens, out.shape[2]), F32)
    tails = [
        jnp.concatenate([dq_sum[x * tokens : (x + 1) * tokens], rest], axis=0).astype(BF16)
        for x in range(GROUPS)
    ]
    for b in range(near.shape[0]):
        for z in range(2):
            for kind in range(2):
                total = near[b, z, kind].astype(F32) + from_core[b, z, kind].astype(F32)
                out[2 * b + z, kind * share : (kind + 1) * share] = total.astype(BF16)
            out[2 * b + z, 2 * share :] = tails[b % GROUPS]


def unpack_terms(place, terms, grad_queries, grad_keys, grad_values):
    share, tokens = grad_keys.shape[1], grad_queries.shape[1]
    width = terms.shape[2]
    for x in range(GROUPS):
        cols = slice(x * width, (x + 1) * width)
        sources = [s for s in range(terms.shape[0]) if s // 2 % GROUPS == x]
        for kind, out in enumerate((grad_keys, grad_values)):
            part = slice(kind * share, (kind + 1) * share)
            total = terms[sources[0], part].astype(F32)
            for s in sources[1:]:
                total = total + terms[s, part].astype(F32)
            out[0, :, cols] = total.astype(BF16)
        mine = terms[(place[1] * GROUPS + x) * 2 + place[2], 2 * share :].astype(F32)
        grad_queries[0, :, cols] = mine[:tokens].astype(BF16)


def on_device(sizes, queries, grad_out, attn_out, lse, keys, values, frame_ids, counts):
    low_y, x = lax.axis_index("yl"), lax.axis_index("x")
    high_z, low_z = lax.axis_index("zh"), lax.axis_index("zl")
    high_y, core = lax.axis_index("yh"), lax.axis_index("c")
    tokens_here = queries.shape[1]
    heads = lse.shape[2] // GROUPS
    width = heads * HS
    frame_tokens = keys.shape[1]
    spread = sizes["zh"] * sizes["yh"]
    members = GROUPS * spread
    blocks_q = sizes["yl"] * sizes["x"]
    share = frame_tokens // blocks_q

    def memory_frame(z, c):
        return ((high_z * 2 + z) * sizes["yh"] + high_y) * 2 + c

    group = [(low_z, core), (low_z, 1 - core), (1 - low_z, core), (1 - low_z, 1 - core)]
    place = jnp.stack(
        [x, low_y, low_z]
        + [memory_frame(z, c) for z, c in group]
        + [z * 2 + c for z, c in group]
    ).astype(jnp.int32)

    kv = jnp.stack(
        [lax.dynamic_slice_in_dim(a[0], x * width, width, 1) for a in (keys, values)]
    )
    kv = lax.all_gather(kv, ("zl", "c"), axis=0, tiled=False)

    packed = call(
        functools.partial(pack_rows, heads=heads),
        "pack_rows",
        jax.ShapeDtypeStruct((members, tokens_here, 2 * width + LANES), BF16),
        [IN_SMEM] + [IN_VMEM] * 4,
        place,
        queries,
        grad_out,
        attn_out,
        lse,
    )
    rows = lax.all_to_all(packed, ("zh", "yh", "x"), 0, 0, tiled=True)
    rows = rows.reshape(members * tokens_here, -1)

    part = jax.ShapeDtypeStruct((blocks_q, 2, 2, share, width), BF16)
    dq, near, far = call(
        functools.partial(attention_grads, heads=heads),
        "attention_grads",
        (jax.ShapeDtypeStruct((rows.shape[0], width), BF16), part, part),
        [IN_SMEM] * 2 + [IN_VMEM] * 3,
        place,
        counts,
        frame_ids,
        rows,
        kv,
    )

    dq = lax.all_to_all(
        dq.reshape(spread, GROUPS * tokens_here, width), ("zh", "yh"), 0, 0, tiled=True
    )
    flip = [(0, 1), (1, 0)]
    from_core = lax.ppermute(far, "c", flip)
    terms = call(
        pack_terms,
        "pack_terms",
        jax.ShapeDtypeStruct((blocks_q * 2, 2 * share + 2 * tokens_here, width), BF16),
        [IN_VMEM] * 3,
        dq,
        near,
        from_core,
    )
    terms = lax.all_to_all(terms, ("yl", "x", "zl"), 0, 0, tiled=True)
    return call(
        unpack_terms,
        "unpack_terms",
        (
            jax.ShapeDtypeStruct(queries.shape, BF16),
            jax.ShapeDtypeStruct((1, share, keys.shape[2]), BF16),
            jax.ShapeDtypeStruct((1, share, keys.shape[2]), BF16),
        ),
        [IN_SMEM, IN_VMEM],
        place,
        terms,
    )


def solution(mesh):
    query, mem = mesh.shape["query"], mesh.shape["mem"]
    sizes = {"yl": query // GROUPS, "x": GROUPS, "zh": mem // 16, "zl": 2, "yh": 4, "c": 2}
    if mem < 16:
        sizes.update(zh=1, yh=mem // 4)
    fine = Mesh(mesh.devices.reshape(tuple(sizes.values())), tuple(sizes))
    q_axes, m_axes = ("yl", "x"), ("zh", "zl", "yh", "c")
    rows = P(q_axes, m_axes, None)
    frames = P(m_axes, None, None)
    return jax.shard_map(
        functools.partial(on_device, sizes),
        mesh=fine,
        in_specs=(rows, rows, rows, rows, frames, frames, P(), P()),
        out_specs=(rows, P(m_axes, q_axes, None), P(m_axes, q_axes, None)),
        check_vma=False,
    )
```

```python
import functools
import math

import jax
import jax.numpy as jnp
from jax import lax
from jax.experimental import pallas as pl
from jax.experimental.pallas import tpu as pltpu
from jax.sharding import Mesh, PartitionSpec as P

HS = 128
GROUPS = 4
LANES = 128
MASKED = -1e30
F32, BF16 = jnp.float32, jnp.bfloat16
IN_VMEM = pl.BlockSpec(memory_space=pltpu.VMEM)
IN_SMEM = pl.BlockSpec(memory_space=pltpu.SMEM)
LONG = pl.CostEstimate(flops=10**11, bytes_accessed=10**6, transcendentals=0)


def call(body, name, out_shape, in_specs, *args, cost=None):
    return pl.pallas_call(
        body,
        out_shape=out_shape,
        in_specs=in_specs,
        cost_estimate=cost,
        out_specs=jax.tree.map(lambda _: IN_VMEM, out_shape),
        compiler_params=pltpu.CompilerParams(vmem_limit_bytes=40 * 2**20),
        name=name,
    )(*args)


def pack_rows(place, queries, grad_out, attn_out, lse, out, *, heads):
    width = heads * HS
    tokens = queries.shape[1]
    lane = lax.broadcasted_iota(jnp.int32, (tokens, LANES), 1)
    lse_scaled = lse[0] * HS**0.5
    for group in range(GROUPS):
        extra = jnp.where(lane == 4 * heads + place[0], 1.0, 0.0).astype(F32)
        for h in range(heads):
            head = group * heads + h
            cols = slice(head * HS, (head + 1) * HS)
            product = grad_out[0, :, cols].astype(F32) * attn_out[0, :, cols].astype(F32)
            delta = jnp.sum(product, axis=1, keepdims=True)
            for i, value in enumerate((lse_scaled[:, head : head + 1], delta)):
                high = value.astype(BF16).astype(F32)
                extra = jnp.where(lane == 2 * i * heads + h, high, extra)
                extra = jnp.where(lane == (2 * i + 1) * heads + h, value - high, extra)
        cols = slice(group * width, (group + 1) * width)
        row = jnp.concatenate(
            [queries[0, :, cols], grad_out[0, :, cols], extra.astype(BF16)], axis=1
        )
        for s in range(out.shape[0] // GROUPS):
            out[s * GROUPS + group] = row


def pair_frames(kv_own, kv_far, out):
    out[0] = kv_own[...]
    out[1] = kv_far[...]


def frame_columns(kv_own, kv_core, kind, cols):
    blocks = (kv_own.at[0], kv_core.at[0], kv_own.at[1], kv_core.at[1])
    return jnp.concatenate([b[kind, :, cols] for b in blocks], axis=0)


def key_value_grads(
    place, amounts, ids, rows, kv_own, kv_core, grad_scores, near, far, *, heads
):
    score_scale = HS ** (-0.5)
    exponent_scale = score_scale * math.log2(math.e)
    width = heads * HS
    tokens = kv_own.shape[2]

    frame = lax.broadcasted_iota(jnp.int32, ids.shape, 0)
    entry = lax.broadcasted_iota(jnp.int32, ids.shape, 1)
    limit = jnp.zeros(ids.shape, jnp.int32)
    for f in range(ids.shape[0]):
        limit = jnp.where(frame == f, amounts[f], limit)
    listed = entry < limit
    row8 = lax.broadcasted_iota(jnp.int32, (ids.shape[0], LANES), 0) - place[1] * GROUPS
    lane8 = lax.broadcasted_iota(jnp.int32, (ids.shape[0], LANES), 1)
    spot = (lane8 == 4 * heads + row8) & (row8 >= 0) & (row8 < GROUPS)
    biases = []
    for d in range(4):
        hit = jnp.where((ids[...] == place[2 + d]) & listed, 1.0, 0.0)
        found = jnp.max(hit, axis=1, keepdims=True)
        bias = jnp.sum(jnp.where(spot, (1.0 - found) * MASKED, 0.0), axis=0, keepdims=True)
        biases.append(jnp.broadcast_to(bias, (tokens, LANES)))
    bias_all = jnp.concatenate(biases, axis=0)
    lane = lax.broadcasted_iota(jnp.int32, bias_all.shape, 1)
    extra = rows[:, 2 * width :]

    for h in range(heads):
        cols = slice(h * HS, (h + 1) * HS)
        q = rows[:, cols]
        g = rows[:, width + h * HS : width + (h + 1) * HS]
        k = frame_columns(kv_own, kv_core, 0, cols)
        v = frame_columns(kv_own, kv_core, 1, cols)
        k_pick = jnp.where((lane == h) | (lane == heads + h), -1.0, bias_all).astype(BF16)
        v_pick = jnp.where((lane == 2 * heads + h) | (lane == 3 * heads + h), -1.0, 0.0).astype(BF16)
        contract = (((1,), (1,)), ((), ()))
        scores = lax.dot_general(
            jnp.concatenate([k, k_pick], axis=1),
            jnp.concatenate([q, extra], axis=1),
            contract,
            preferred_element_type=F32,
        )
        probs = jnp.exp2(scores * exponent_scale)
        grad_probs = lax.dot_general(
            jnp.concatenate([v, v_pick], axis=1),
            jnp.concatenate([g, extra], axis=1),
            contract,
            preferred_element_type=F32,
        )
        ds = (probs * grad_probs).astype(BF16)
        grad_scores[h] = ds
        dv = jnp.dot(probs.astype(BF16), g, preferred_element_type=F32).astype(BF16)
        dk = (jnp.dot(ds, q, preferred_element_type=F32) * score_scale).astype(BF16)
        for d, out in enumerate((near, far, near, far)):
            part = slice(d * tokens, (d + 1) * tokens)
            piece = (out.shape[1], out.shape[3], HS)
            out[d // 2, :, 0, :, cols] = dk[part].reshape(piece)
            out[d // 2, :, 1, :, cols] = dv[part].reshape(piece)


def query_grads(grad_scores, kv_own, kv_core, dq):
    for h in range(grad_scores.shape[0]):
        cols = slice(h * HS, (h + 1) * HS)
        k = frame_columns(kv_own, kv_core, 0, cols)
        dq_h = lax.dot_general(
            grad_scores[h], k, (((0,), (0,)), ((), ())), preferred_element_type=F32
        )
        dq[:, cols] = (dq_h * HS ** (-0.5)).astype(BF16)


def add_core(near, from_core, out):
    out[...] = (near[1].astype(F32) + from_core[1].astype(F32)).astype(BF16)


def add_far(near, from_core, from_far, out):
    total = near[0].astype(F32) + from_core[0].astype(F32)
    out[...] = (total + from_far[...].astype(F32)).astype(BF16)


def pack_terms(dq, part, out):
    share = part.shape[2]
    dq_sum = dq[0].astype(F32)
    for s in range(1, dq.shape[0]):
        dq_sum = dq_sum + dq[s].astype(F32)
    tokens = dq.shape[1] // GROUPS
    for b in range(out.shape[0]):
        for kind in range(2):
            out[b, kind * share : (kind + 1) * share] = part[b, kind]
        x = b % GROUPS
        piece = dq_sum[x * tokens : (x + 1) * tokens]
        rest = jnp.zeros((out.shape[1] - 2 * share - tokens, piece.shape[1]), F32)
        out[b, 2 * share :] = jnp.concatenate([piece, rest], axis=0).astype(BF16)


def unpack_terms(place, terms, grad_queries, grad_keys, grad_values):
    share, tokens = grad_keys.shape[1], grad_queries.shape[1]
    width = terms.shape[2]
    for x in range(GROUPS):
        cols = slice(x * width, (x + 1) * width)
        for kind, out in enumerate((grad_keys, grad_values)):
            part = slice(kind * share, (kind + 1) * share)
            total = terms[x, part].astype(F32)
            for y in range(1, terms.shape[0] // GROUPS):
                total = total + terms[y * GROUPS + x, part].astype(F32)
            out[0, :, cols] = total.astype(BF16)
        mine = terms[place[1] * GROUPS + x, 2 * share :].astype(F32)
        grad_queries[0, :, cols] = mine[:tokens].astype(BF16)


def on_device(sizes, queries, grad_out, attn_out, lse, keys, values, frame_ids, counts):
    low_y, x, z = (lax.axis_index(a) for a in ("yl", "x", "z"))
    far_y, near_y, core = (lax.axis_index(a) for a in ("yf", "ym", "c"))
    tokens_here = queries.shape[1]
    heads = lse.shape[2] // GROUPS
    width = heads * HS
    frame_tokens = keys.shape[1]
    spread = sizes["z"] * sizes["ym"]
    members = GROUPS * spread
    blocks_q = sizes["yl"] * sizes["x"]
    share = frame_tokens // blocks_q

    def memory_frame(far, c):
        return ((z * 2 + far) * sizes["ym"] + near_y) * 2 + c

    place = jnp.stack(
        [
            x,
            low_y,
            memory_frame(far_y, core),
            memory_frame(far_y, 1 - core),
            memory_frame(1 - far_y, core),
            memory_frame(1 - far_y, 1 - core),
        ]
    ).astype(jnp.int32)

    flip = [(0, 1), (1, 0)]
    kv = jnp.stack(
        [lax.dynamic_slice_in_dim(a[0], x * width, width, 1) for a in (keys, values)]
    )
    kv_far = lax.ppermute(kv, "yf", flip)
    kv_own = call(
        pair_frames,
        "pair_frames",
        jax.ShapeDtypeStruct((2,) + kv.shape, BF16),
        [IN_VMEM] * 2,
        kv,
        kv_far,
        cost=LONG,
    )
    kv_core = lax.ppermute(kv_own, "c", flip)

    packed = call(
        functools.partial(pack_rows, heads=heads),
        "pack_rows",
        jax.ShapeDtypeStruct((members, tokens_here, 2 * width + LANES), BF16),
        [IN_SMEM] + [IN_VMEM] * 4,
        place,
        queries,
        grad_out,
        attn_out,
        lse,
    )
    rows = lax.all_to_all(packed, ("z", "ym", "x"), 0, 0, tiled=True)
    rows = rows.reshape(members * tokens_here, -1)

    part = jax.ShapeDtypeStruct((2, blocks_q, 2, share, width), BF16)
    half = jax.ShapeDtypeStruct(part.shape[1:], BF16)
    grad_scores, near, far = call(
        functools.partial(key_value_grads, heads=heads),
        "key_value_grads",
        (jax.ShapeDtypeStruct((heads, 4 * frame_tokens, rows.shape[0]), BF16), part, part),
        [IN_SMEM] * 2 + [IN_VMEM] * 4,
        place,
        counts,
        frame_ids,
        rows,
        kv_own,
        kv_core,
    )

    from_core = lax.ppermute(far, "c", flip)
    dq = call(
        query_grads,
        "query_grads",
        jax.ShapeDtypeStruct((rows.shape[0], width), BF16),
        [IN_VMEM] * 3,
        grad_scores,
        kv_own,
        kv_core,
    )
    from_core, dq = lax.optimization_barrier((from_core, dq))
    other = call(add_core, "add_core", half, [IN_VMEM] * 2, near, from_core)
    from_far = lax.ppermute(other, "yf", flip)
    mine = call(
        add_far, "add_far", half, [IN_VMEM] * 3, near, from_core, from_far, cost=LONG
    )
    dq = lax.all_to_all(
        dq.reshape(spread, GROUPS * tokens_here, width), ("z", "ym"), 0, 0, tiled=True
    )
    terms = call(
        pack_terms,
        "pack_terms",
        jax.ShapeDtypeStruct((blocks_q, 2 * share + 2 * tokens_here, width), BF16),
        [IN_VMEM] * 2,
        dq,
        mine,
    )
    terms = lax.all_to_all(terms, ("yl", "x"), 0, 0, tiled=True)
    return call(
        unpack_terms,
        "unpack_terms",
        (
            jax.ShapeDtypeStruct(queries.shape, BF16),
            jax.ShapeDtypeStruct((1, share, keys.shape[2]), BF16),
            jax.ShapeDtypeStruct((1, share, keys.shape[2]), BF16),
        ),
        [IN_SMEM, IN_VMEM],
        place,
        terms,
    )


def solution(mesh):
    query, mem = mesh.shape["query"], mesh.shape["mem"]
    sizes = {"yl": query // GROUPS, "x": GROUPS, "z": mem // 8, "yf": 2, "ym": 2, "c": 2}
    if mem < 8:
        sizes.update(z=1, ym=mem // 4)
    fine = Mesh(mesh.devices.reshape(tuple(sizes.values())), tuple(sizes))
    q_axes, m_axes = ("yl", "x"), ("z", "yf", "ym", "c")
    rows = P(q_axes, m_axes, None)
    frames = P(m_axes, None, None)
    return jax.shard_map(
        functools.partial(on_device, sizes),
        mesh=fine,
        in_specs=(rows, rows, rows, rows, frames, frames, P(), P()),
        out_specs=(rows, P(m_axes, q_axes, None), P(m_axes, q_axes, None)),
        check_vma=False,
    )
```

```python
import functools
import math

import jax
import jax.numpy as jnp
from jax import lax
from jax.experimental import pallas as pl
from jax.experimental.pallas import tpu as pltpu
from jax.sharding import Mesh, PartitionSpec as P

HS = 128
GROUPS = 4
LANES = 128
MASKED = -1e30
F32, BF16 = jnp.float32, jnp.bfloat16
IN_VMEM = pl.BlockSpec(memory_space=pltpu.VMEM)
IN_SMEM = pl.BlockSpec(memory_space=pltpu.SMEM)
LONG = pl.CostEstimate(flops=10**11, bytes_accessed=10**6, transcendentals=0)


def call(body, name, out_shape, in_specs, *args, cost=None):
    return pl.pallas_call(
        body,
        out_shape=out_shape,
        in_specs=in_specs,
        cost_estimate=cost,
        out_specs=jax.tree.map(lambda _: IN_VMEM, out_shape),
        compiler_params=pltpu.CompilerParams(vmem_limit_bytes=20 * 2**20),
        name=name,
    )(*args)


def pack_rows(place, queries, grad_out, attn_out, lse, out, *, heads):
    width = heads * HS
    tokens = queries.shape[1]
    lane = lax.broadcasted_iota(jnp.int32, (tokens, LANES), 1)
    lse_scaled = lse[0] * HS**0.5
    for group in range(GROUPS):
        extra = jnp.where(lane == 4 * heads + place[0], 1.0, 0.0).astype(F32)
        for h in range(heads):
            head = group * heads + h
            cols = slice(head * HS, (head + 1) * HS)
            product = grad_out[0, :, cols].astype(F32) * attn_out[0, :, cols].astype(F32)
            delta = jnp.sum(product, axis=1, keepdims=True)
            for i, value in enumerate((lse_scaled[:, head : head + 1], delta)):
                high = value.astype(BF16).astype(F32)
                extra = jnp.where(lane == 2 * i * heads + h, high, extra)
                extra = jnp.where(lane == (2 * i + 1) * heads + h, value - high, extra)
        cols = slice(group * width, (group + 1) * width)
        row = jnp.concatenate(
            [queries[0, :, cols], grad_out[0, :, cols], extra.astype(BF16)], axis=1
        )
        for s in range(out.shape[0] // GROUPS):
            out[s * GROUPS + group] = row


def pair_frames(kv_own, kv_z, out):
    out[0] = kv_own[...]
    out[1] = kv_z[...]


def attention_grads(
    place, amounts, ids, rows, kv_own, kv_core, dq, near, far_keys, far_values, *, heads
):
    score_scale = HS ** (-0.5)
    exponent_scale = score_scale * math.log2(math.e)
    width = heads * HS
    blocks = (kv_own.at[0], kv_core.at[0], kv_own.at[1], kv_core.at[1])
    tokens = kv_own.shape[2]

    frame = lax.broadcasted_iota(jnp.int32, ids.shape, 0)
    entry = lax.broadcasted_iota(jnp.int32, ids.shape, 1)
    limit = jnp.zeros(ids.shape, jnp.int32)
    for f in range(ids.shape[0]):
        limit = jnp.where(frame == f, amounts[f], limit)
    listed = entry < limit
    row8 = lax.broadcasted_iota(jnp.int32, (ids.shape[0], LANES), 0) - place[1] * GROUPS
    lane8 = lax.broadcasted_iota(jnp.int32, (ids.shape[0], LANES), 1)
    spot = (lane8 == 4 * heads + row8) & (row8 >= 0) & (row8 < GROUPS)
    biases = []
    for d in range(4):
        hit = jnp.where((ids[...] == place[2 + d]) & listed, 1.0, 0.0)
        found = jnp.max(hit, axis=1, keepdims=True)
        bias = jnp.sum(jnp.where(spot, (1.0 - found) * MASKED, 0.0), axis=0, keepdims=True)
        biases.append(jnp.broadcast_to(bias, (tokens, LANES)))
    bias_all = jnp.concatenate(biases, axis=0)
    lane = lax.broadcasted_iota(jnp.int32, bias_all.shape, 1)
    extra = rows[:, 2 * width :]

    for h in range(heads):
        cols = slice(h * HS, (h + 1) * HS)
        q = rows[:, cols]
        g = rows[:, width + h * HS : width + (h + 1) * HS]
        k = jnp.concatenate([b[0, :, cols] for b in blocks], axis=0)
        v = jnp.concatenate([b[1, :, cols] for b in blocks], axis=0)
        k_pick = jnp.where((lane == h) | (lane == heads + h), -1.0, bias_all).astype(BF16)
        v_pick = jnp.where((lane == 2 * heads + h) | (lane == 3 * heads + h), -1.0, 0.0).astype(BF16)
        contract = (((1,), (1,)), ((), ()))
        scores = lax.dot_general(
            jnp.concatenate([k, k_pick], axis=1),
            jnp.concatenate([q, extra], axis=1),
            contract,
            preferred_element_type=F32,
        )
        probs = jnp.exp2(scores * exponent_scale)
        grad_probs = lax.dot_general(
            jnp.concatenate([v, v_pick], axis=1),
            jnp.concatenate([g, extra], axis=1),
            contract,
            preferred_element_type=F32,
        )
        grad_scores = (probs * grad_probs).astype(BF16)
        dv = jnp.dot(probs.astype(BF16), g, preferred_element_type=F32).astype(BF16)
        dk = (jnp.dot(grad_scores, q, preferred_element_type=F32) * score_scale).astype(BF16)
        dq_h = lax.dot_general(
            grad_scores, k, (((0,), (0,)), ((), ())), preferred_element_type=F32
        )
        dq[:, cols] = (dq_h * score_scale).astype(BF16)
        piece = (near.shape[0], near.shape[3], HS)
        for d in range(4):
            part = slice(d * tokens, (d + 1) * tokens)
            z = place[6] if d < 2 else 1 - place[6]
            if d % 2 == 0:
                near[:, z, 0, :, cols] = dk[part].reshape(piece)
                near[:, z, 1, :, cols] = dv[part].reshape(piece)
            else:
                far_keys[:, z, :, cols] = dk[part].reshape(piece)
                far_values[:, z, :, cols] = dv[part].reshape(piece)


def pack_terms(dq, near, core_keys, core_values, out):
    share = near.shape[3]
    dq_sum = dq[0].astype(F32)
    for s in range(1, dq.shape[0]):
        dq_sum = dq_sum + dq[s].astype(F32)
    tokens = dq.shape[1] // GROUPS
    rest = jnp.zeros((out.shape[1] - 2 * share - tokens, out.shape[2]), F32)
    tails = [
        jnp.concatenate([dq_sum[x * tokens : (x + 1) * tokens], rest], axis=0).astype(BF16)
        for x in range(GROUPS)
    ]
    for b in range(near.shape[0]):
        for z in range(2):
            for kind, other in enumerate((core_keys, core_values)):
                total = near[b, z, kind].astype(F32) + other[b, z].astype(F32)
                out[2 * b + z, kind * share : (kind + 1) * share] = total.astype(BF16)
            out[2 * b + z, 2 * share :] = tails[b % GROUPS]


def unpack_terms(place, terms, grad_queries, grad_keys, grad_values):
    share, tokens = grad_keys.shape[1], grad_queries.shape[1]
    width = terms.shape[2]
    for x in range(GROUPS):
        cols = slice(x * width, (x + 1) * width)
        sources = [s for s in range(terms.shape[0]) if s // 2 % GROUPS == x]
        for kind, out in enumerate((grad_keys, grad_values)):
            part = slice(kind * share, (kind + 1) * share)
            total = terms[sources[0], part].astype(F32)
            for s in sources[1:]:
                total = total + terms[s, part].astype(F32)
            out[0, :, cols] = total.astype(BF16)
        mine = terms[(place[1] * GROUPS + x) * 2 + place[6], 2 * share :].astype(F32)
        grad_queries[0, :, cols] = mine[:tokens].astype(BF16)


def on_device(sizes, queries, grad_out, attn_out, lse, keys, values, frame_ids, counts):
    low_y, x, high_z = (lax.axis_index(a) for a in ("yl", "x", "zh"))
    low_z, high_y, core = (lax.axis_index(a) for a in ("zl", "yh", "c"))
    tokens_here = queries.shape[1]
    heads = lse.shape[2] // GROUPS
    width = heads * HS
    frame_tokens = keys.shape[1]
    spread = sizes["zh"] * sizes["yh"]
    members = GROUPS * spread
    blocks_q = sizes["yl"] * sizes["x"]
    share = frame_tokens // blocks_q

    def memory_frame(z, c):
        return ((high_z * 2 + z) * sizes["yh"] + high_y) * 2 + c

    place = jnp.stack(
        [
            x,
            low_y,
            memory_frame(low_z, core),
            memory_frame(low_z, 1 - core),
            memory_frame(1 - low_z, core),
            memory_frame(1 - low_z, 1 - core),
            low_z,
        ]
    ).astype(jnp.int32)

    flip = [(0, 1), (1, 0)]
    kv = jnp.stack(
        [lax.dynamic_slice_in_dim(a[0], x * width, width, 1) for a in (keys, values)]
    )
    kv_z = lax.ppermute(kv, "zl", flip)
    kv_own = call(
        pair_frames,
        "pair_frames",
        jax.ShapeDtypeStruct((2,) + kv.shape, BF16),
        [IN_VMEM] * 2,
        kv,
        kv_z,
        cost=LONG,
    )
    kv_core = lax.ppermute(kv_own, "c", flip)

    packed = call(
        functools.partial(pack_rows, heads=heads),
        "pack_rows",
        jax.ShapeDtypeStruct((members, tokens_here, 2 * width + LANES), BF16),
        [IN_SMEM] + [IN_VMEM] * 4,
        place,
        queries,
        grad_out,
        attn_out,
        lse,
    )
    rows = lax.all_to_all(packed, ("zh", "yh", "x"), 0, 0, tiled=True)
    rows = rows.reshape(members * tokens_here, -1)

    part = jax.ShapeDtypeStruct((blocks_q, 2, 2, share, width), BF16)
    half = jax.ShapeDtypeStruct((blocks_q, 2, share, width), BF16)
    dq, near, *far = call(
        functools.partial(attention_grads, heads=heads),
        "attention_grads",
        (jax.ShapeDtypeStruct((rows.shape[0], width), BF16), part, half, half),
        [IN_SMEM] * 2 + [IN_VMEM] * 4,
        place,
        counts,
        frame_ids,
        rows,
        kv_own,
        kv_core,
    )

    dq = lax.all_to_all(
        dq.reshape(spread, GROUPS * tokens_here, width), ("zh", "yh"), 0, 0, tiled=True
    )
    from_core = [lax.ppermute(a, "c", flip) for a in far]
    terms = call(
        pack_terms,
        "pack_terms",
        jax.ShapeDtypeStruct((blocks_q * 2, 2 * share + 2 * tokens_here, width), BF16),
        [IN_VMEM] * 4,
        dq,
        near,
        *from_core,
    )
    terms = lax.all_to_all(terms, ("yl", "x", "zl"), 0, 0, tiled=True)
    return call(
        unpack_terms,
        "unpack_terms",
        (
            jax.ShapeDtypeStruct(queries.shape, BF16),
            jax.ShapeDtypeStruct((1, share, keys.shape[2]), BF16),
            jax.ShapeDtypeStruct((1, share, keys.shape[2]), BF16),
        ),
        [IN_SMEM, IN_VMEM],
        place,
        terms,
    )


def solution(mesh):
    query, mem = mesh.shape["query"], mesh.shape["mem"]
    sizes = {"yl": query // GROUPS, "x": GROUPS, "zh": mem // 16, "zl": 2, "yh": 4, "c": 2}
    if mem < 16:
        sizes.update(zh=1, yh=mem // 4)
    fine = Mesh(mesh.devices.reshape(tuple(sizes.values())), tuple(sizes))
    q_axes, m_axes = ("yl", "x"), ("zh", "zl", "yh", "c")
    rows = P(q_axes, m_axes, None)
    frames = P(m_axes, None, None)
    return jax.shard_map(
        functools.partial(on_device, sizes),
        mesh=fine,
        in_specs=(rows, rows, rows, rows, frames, frames, P(), P()),
        out_specs=(rows, P(m_axes, q_axes, None), P(m_axes, q_axes, None)),
        check_vma=False,
    )
```

```python
import functools
import math

import jax
import jax.numpy as jnp
from jax import lax
from jax.experimental import pallas as pl
from jax.experimental.pallas import tpu as pltpu
from jax.sharding import Mesh, PartitionSpec as P

HS = 128
GROUPS = 4
LANES = 128
MASKED = -1e30
F32, BF16 = jnp.float32, jnp.bfloat16
IN_VMEM = pl.BlockSpec(memory_space=pltpu.VMEM)
IN_SMEM = pl.BlockSpec(memory_space=pltpu.SMEM)
LONG = pl.CostEstimate(flops=10**11, bytes_accessed=10**6, transcendentals=0)


def call(body, name, out_shape, in_specs, *args, cost=None):
    return pl.pallas_call(
        body,
        out_shape=out_shape,
        in_specs=in_specs,
        cost_estimate=cost,
        out_specs=jax.tree.map(lambda _: IN_VMEM, out_shape),
        compiler_params=pltpu.CompilerParams(vmem_limit_bytes=20 * 2**20),
        name=name,
    )(*args)


def pack_rows(place, queries, grad_out, attn_out, lse, out, *, heads):
    width = heads * HS
    tokens = queries.shape[1]
    lane = lax.broadcasted_iota(jnp.int32, (tokens, LANES), 1)
    lse_scaled = lse[0] * HS**0.5
    for group in range(GROUPS):
        extra = jnp.where(lane == 4 * heads + place[0], 1.0, 0.0).astype(F32)
        for h in range(heads):
            head = group * heads + h
            cols = slice(head * HS, (head + 1) * HS)
            product = grad_out[0, :, cols].astype(F32) * attn_out[0, :, cols].astype(F32)
            delta = jnp.sum(product, axis=1, keepdims=True)
            for i, value in enumerate((lse_scaled[:, head : head + 1], delta)):
                high = value.astype(BF16).astype(F32)
                extra = jnp.where(lane == 2 * i * heads + h, high, extra)
                extra = jnp.where(lane == (2 * i + 1) * heads + h, value - high, extra)
        cols = slice(group * width, (group + 1) * width)
        row = jnp.concatenate(
            [queries[0, :, cols], grad_out[0, :, cols], extra.astype(BF16)], axis=1
        )
        for s in range(out.shape[0] // GROUPS):
            out[s * GROUPS + group] = row


def pair_frames(kv_own, kv_z, out):
    out[0] = kv_own[...]
    out[1] = kv_z[...]


def attention_grads(
    place, amounts, ids, rows, kv_own, kv_core, dq, near, far_keys, far_values, *, heads
):
    score_scale = HS ** (-0.5)
    exponent_scale = score_scale * math.log2(math.e)
    width = heads * HS
    blocks = (kv_own.at[0], kv_core.at[0], kv_own.at[1], kv_core.at[1])
    tokens = kv_own.shape[2]

    frame = lax.broadcasted_iota(jnp.int32, ids.shape, 0)
    entry = lax.broadcasted_iota(jnp.int32, ids.shape, 1)
    limit = jnp.zeros(ids.shape, jnp.int32)
    for f in range(ids.shape[0]):
        limit = jnp.where(frame == f, amounts[f], limit)
    listed = entry < limit
    row8 = lax.broadcasted_iota(jnp.int32, (ids.shape[0], LANES), 0)
    lane8 = lax.broadcasted_iota(jnp.int32, (ids.shape[0], LANES), 1)
    slot = (row8 >> 2) * 2 + (row8 & 1)
    spot = (lane8 == 4 * heads + slot) & (((row8 >> 1) & 1) == place[1])
    biases = []
    for d in range(4):
        hit = jnp.where((ids[...] == place[2 + d]) & listed, 1.0, 0.0)
        found = jnp.max(hit, axis=1, keepdims=True)
        bias = jnp.sum(jnp.where(spot, (1.0 - found) * MASKED, 0.0), axis=0, keepdims=True)
        biases.append(jnp.broadcast_to(bias, (tokens, LANES)))
    bias_all = jnp.concatenate(biases, axis=0)
    lane = lax.broadcasted_iota(jnp.int32, bias_all.shape, 1)
    extra = rows[:, 2 * width :]

    for h in range(heads):
        cols = slice(h * HS, (h + 1) * HS)
        q = rows[:, cols]
        g = rows[:, width + h * HS : width + (h + 1) * HS]
        k = jnp.concatenate([b[0, :, cols] for b in blocks], axis=0)
        v = jnp.concatenate([b[1, :, cols] for b in blocks], axis=0)
        k_pick = jnp.where((lane == h) | (lane == heads + h), -1.0, bias_all).astype(BF16)
        v_pick = jnp.where((lane == 2 * heads + h) | (lane == 3 * heads + h), -1.0, 0.0).astype(BF16)
        contract = (((1,), (1,)), ((), ()))
        scores = lax.dot_general(
            jnp.concatenate([k, k_pick], axis=1),
            jnp.concatenate([q, extra], axis=1),
            contract,
            preferred_element_type=F32,
        )
        probs = jnp.exp2(scores * exponent_scale)
        grad_probs = lax.dot_general(
            jnp.concatenate([v, v_pick], axis=1),
            jnp.concatenate([g, extra], axis=1),
            contract,
            preferred_element_type=F32,
        )
        grad_scores = (probs * grad_probs).astype(BF16)
        dv = jnp.dot(probs.astype(BF16), g, preferred_element_type=F32).astype(BF16)
        dk = (jnp.dot(grad_scores, q, preferred_element_type=F32) * score_scale).astype(BF16)
        dq_h = lax.dot_general(
            grad_scores, k, (((0,), (0,)), ((), ())), preferred_element_type=F32
        )
        dq[:, cols] = (dq_h * score_scale).astype(BF16)
        piece = (near.shape[0], near.shape[3], HS)
        for d in range(4):
            part = slice(d * tokens, (d + 1) * tokens)
            z = place[6] if d < 2 else 1 - place[6]
            if d % 2 == 0:
                near[:, z, 0, :, cols] = dk[part].reshape(piece)
                near[:, z, 1, :, cols] = dv[part].reshape(piece)
            else:
                far_keys[:, z, :, cols] = dk[part].reshape(piece)
                far_values[:, z, :, cols] = dv[part].reshape(piece)


def pack_terms(dq, near, core_keys, core_values, out):
    share = near.shape[3]
    dq_sum = dq[0].astype(F32)
    for s in range(1, dq.shape[0]):
        dq_sum = dq_sum + dq[s].astype(F32)
    tokens = dq.shape[1] // GROUPS
    rest = jnp.zeros((out.shape[1] - 2 * share - tokens, out.shape[2]), F32)
    tails = [
        jnp.concatenate([dq_sum[x * tokens : (x + 1) * tokens], rest], axis=0).astype(BF16)
        for x in range(GROUPS)
    ]
    for b in range(near.shape[0]):
        for z in range(2):
            for kind, other in enumerate((core_keys, core_values)):
                total = near[b, z, kind].astype(F32) + other[b, z].astype(F32)
                out[2 * b + z, kind * share : (kind + 1) * share] = total.astype(BF16)
            out[2 * b + z, 2 * share :] = tails[b // 4 * 2 + b % 2]


def unpack_terms(place, terms, grad_queries, grad_keys, grad_values):
    share, tokens = grad_keys.shape[1], grad_queries.shape[1]
    width = terms.shape[2]
    for group in range(GROUPS):
        cols = slice(group * width, (group + 1) * width)
        first = group // 2 * 8 + group % 2 * 2
        sources = [first + 4 * x + z for x in range(2) for z in range(2)]
        for kind, out in enumerate((grad_keys, grad_values)):
            part = slice(kind * share, (kind + 1) * share)
            total = terms[sources[0], part].astype(F32)
            for s in sources[1:]:
                total = total + terms[s, part].astype(F32)
            out[0, :, cols] = total.astype(BF16)
        mine = terms[first + 4 * place[1] + place[6], 2 * share :].astype(F32)
        grad_queries[0, :, cols] = mine[:tokens].astype(BF16)


def on_device(sizes, queries, grad_out, attn_out, lse, keys, values, frame_ids, counts):
    low_y, high_x, low_x, high_z = (lax.axis_index(a) for a in ("yl", "xh", "xl", "zh"))
    low_z, high_y, core = (lax.axis_index(a) for a in ("zl", "yh", "c"))
    tokens_here = queries.shape[1]
    heads = lse.shape[2] // GROUPS
    width = heads * HS
    frame_tokens = keys.shape[1]
    spread = sizes["zh"] * sizes["yh"]
    members = GROUPS * spread
    blocks_q = sizes["yl"] * sizes["xh"] * sizes["xl"]
    share = frame_tokens // blocks_q

    group = low_y * 2 + low_x

    def memory_frame(z, c):
        return ((high_z * 2 + z) * sizes["yh"] + high_y) * 2 + c

    place = jnp.stack(
        [
            group,
            high_x,
            memory_frame(low_z, core),
            memory_frame(low_z, 1 - core),
            memory_frame(1 - low_z, core),
            memory_frame(1 - low_z, 1 - core),
            low_z,
        ]
    ).astype(jnp.int32)

    flip = [(0, 1), (1, 0)]
    kv = jnp.stack(
        [lax.dynamic_slice_in_dim(a[0], group * width, width, 1) for a in (keys, values)]
    )
    kv_z = lax.ppermute(kv, "zl", flip)
    kv_own = call(
        pair_frames,
        "pair_frames",
        jax.ShapeDtypeStruct((2,) + kv.shape, BF16),
        [IN_VMEM] * 2,
        kv,
        kv_z,
        cost=LONG,
    )
    kv_core = lax.ppermute(kv_own, "c", flip)

    packed = call(
        functools.partial(pack_rows, heads=heads),
        "pack_rows",
        jax.ShapeDtypeStruct((members, tokens_here, 2 * width + LANES), BF16),
        [IN_SMEM] + [IN_VMEM] * 4,
        place,
        queries,
        grad_out,
        attn_out,
        lse,
    )
    rows = lax.all_to_all(packed, ("zh", "yh", "yl", "xl"), 0, 0, tiled=True)
    rows = rows.reshape(members * tokens_here, -1)

    part = jax.ShapeDtypeStruct((blocks_q, 2, 2, share, width), BF16)
    half = jax.ShapeDtypeStruct((blocks_q, 2, share, width), BF16)
    dq, near, *far = call(
        functools.partial(attention_grads, heads=heads),
        "attention_grads",
        (jax.ShapeDtypeStruct((rows.shape[0], width), BF16), part, half, half),
        [IN_SMEM] * 2 + [IN_VMEM] * 4,
        place,
        counts,
        frame_ids,
        rows,
        kv_own,
        kv_core,
    )

    dq = lax.all_to_all(
        dq.reshape(spread, GROUPS * tokens_here, width), ("zh", "yh"), 0, 0, tiled=True
    )
    from_core = [lax.ppermute(a, "c", flip) for a in far]
    terms = call(
        pack_terms,
        "pack_terms",
        jax.ShapeDtypeStruct((blocks_q * 2, 2 * share + 2 * tokens_here, width), BF16),
        [IN_VMEM] * 4,
        dq,
        near,
        *from_core,
    )
    terms = lax.all_to_all(terms, ("yl", "xh", "xl", "zl"), 0, 0, tiled=True)
    return call(
        unpack_terms,
        "unpack_terms",
        (
            jax.ShapeDtypeStruct(queries.shape, BF16),
            jax.ShapeDtypeStruct((1, share, keys.shape[2]), BF16),
            jax.ShapeDtypeStruct((1, share, keys.shape[2]), BF16),
        ),
        [IN_SMEM, IN_VMEM],
        place,
        terms,
    )


def solution(mesh):
    query, mem = mesh.shape["query"], mesh.shape["mem"]
    sizes = {"yl": query // 4, "xh": 2, "xl": 2, "zh": mem // 16, "zl": 2, "yh": 4, "c": 2}
    if mem < 16:
        sizes.update(zh=1, yh=mem // 4)
    fine = Mesh(mesh.devices.reshape(tuple(sizes.values())), tuple(sizes))
    q_axes, m_axes = ("yl", "xh", "xl"), ("zh", "zl", "yh", "c")
    rows = P(q_axes, m_axes, None)
    frames = P(m_axes, None, None)
    return jax.shard_map(
        functools.partial(on_device, sizes),
        mesh=fine,
        in_specs=(rows, rows, rows, rows, frames, frames, P(), P()),
        out_specs=(rows, P(m_axes, q_axes, None), P(m_axes, q_axes, None)),
        check_vma=False,
    )
```

```python
import functools
import math

import jax
import jax.numpy as jnp
from jax import lax
from jax.experimental import pallas as pl
from jax.experimental.pallas import tpu as pltpu
from jax.sharding import Mesh, PartitionSpec as P

HS = 128
GROUPS = 4
LANES = 128
MASKED = -1e30
F32, BF16 = jnp.float32, jnp.bfloat16
IN_VMEM = pl.BlockSpec(memory_space=pltpu.VMEM)
IN_SMEM = pl.BlockSpec(memory_space=pltpu.SMEM)
LONG = pl.CostEstimate(flops=10**11, bytes_accessed=10**6, transcendentals=0)


def call(body, name, out_shape, in_specs, *args, cost=None):
    return pl.pallas_call(
        body,
        out_shape=out_shape,
        in_specs=in_specs,
        cost_estimate=cost,
        out_specs=jax.tree.map(lambda _: IN_VMEM, out_shape),
        compiler_params=pltpu.CompilerParams(vmem_limit_bytes=20 * 2**20),
        name=name,
    )(*args)


def pack_rows(place, queries, grad_out, attn_out, lse, out, *, heads):
    width = heads * HS
    tokens = queries.shape[1]
    lane = lax.broadcasted_iota(jnp.int32, (tokens, LANES), 1)
    lse_scaled = lse[0] * HS**0.5
    for group in range(GROUPS):
        extra = jnp.where(lane == 4 * heads + place[0], 1.0, 0.0).astype(F32)
        for h in range(heads):
            head = group * heads + h
            cols = slice(head * HS, (head + 1) * HS)
            product = grad_out[0, :, cols].astype(F32) * attn_out[0, :, cols].astype(F32)
            delta = jnp.sum(product, axis=1, keepdims=True)
            for i, value in enumerate((lse_scaled[:, head : head + 1], delta)):
                high = value.astype(BF16).astype(F32)
                extra = jnp.where(lane == 2 * i * heads + h, high, extra)
                extra = jnp.where(lane == (2 * i + 1) * heads + h, value - high, extra)
        cols = slice(group * width, (group + 1) * width)
        row = jnp.concatenate(
            [queries[0, :, cols], grad_out[0, :, cols], extra.astype(BF16)], axis=1
        )
        for s in range(out.shape[0] // GROUPS):
            out[s * GROUPS + group] = row


def pair_frames(kv_own, kv_z, out):
    out[0] = kv_own[...]
    out[1] = kv_z[...]


def attention_grads(
    place, amounts, ids, rows, kv_own, kv_core, dq, near, far_keys, far_values, *, heads
):
    score_scale = HS ** (-0.5)
    exponent_scale = score_scale * math.log2(math.e)
    width = heads * HS
    blocks = (kv_own.at[0], kv_core.at[0], kv_own.at[1], kv_core.at[1])
    tokens = kv_own.shape[2]

    frame = lax.broadcasted_iota(jnp.int32, ids.shape, 0)
    entry = lax.broadcasted_iota(jnp.int32, ids.shape, 1)
    limit = jnp.zeros(ids.shape, jnp.int32)
    for f in range(ids.shape[0]):
        limit = jnp.where(frame == f, amounts[f], limit)
    listed = entry < limit
    row8 = lax.broadcasted_iota(jnp.int32, (ids.shape[0], LANES), 0)
    lane8 = lax.broadcasted_iota(jnp.int32, (ids.shape[0], LANES), 1)
    slot = (row8 >> 2) * 2 + (row8 & 1)
    spot = (lane8 == 4 * heads + slot) & (((row8 >> 1) & 1) == place[1])
    biases = []
    for d in range(4):
        hit = jnp.where((ids[...] == place[2 + d]) & listed, 1.0, 0.0)
        found = jnp.max(hit, axis=1, keepdims=True)
        bias = jnp.sum(jnp.where(spot, (1.0 - found) * MASKED, 0.0), axis=0, keepdims=True)
        biases.append(bias)
    lane = lax.broadcasted_iota(jnp.int32, (1, LANES), 1)
    extra = rows[:, 2 * width :]

    for h in range(heads):
        cols = slice(h * HS, (h + 1) * HS)
        q = rows[:, cols]
        g = rows[:, width + h * HS : width + (h + 1) * HS]
        k = jnp.concatenate([b[0, :, cols] for b in blocks], axis=0)
        v = jnp.concatenate([b[1, :, cols] for b in blocks], axis=0)
        k_rows = [jnp.where((lane == h) | (lane == heads + h), -1.0, b) for b in biases]
        k_pick = jnp.concatenate(
            [jnp.broadcast_to(r.astype(BF16), (tokens, LANES)) for r in k_rows], axis=0
        )
        v_row = jnp.where((lane == 2 * heads + h) | (lane == 3 * heads + h), -1.0, 0.0)
        v_pick = jnp.broadcast_to(v_row.astype(BF16), k_pick.shape)
        contract = (((1,), (1,)), ((), ()))
        scores = lax.dot_general(
            jnp.concatenate([k, k_pick], axis=1),
            jnp.concatenate([q, extra], axis=1),
            contract,
            preferred_element_type=F32,
        )
        probs = jnp.exp2(scores * exponent_scale)
        grad_probs = lax.dot_general(
            jnp.concatenate([v, v_pick], axis=1),
            jnp.concatenate([g, extra], axis=1),
            contract,
            preferred_element_type=F32,
        )
        grad_scores = (probs * grad_probs).astype(BF16)
        dv = jnp.dot(probs.astype(BF16), g, preferred_element_type=F32).astype(BF16)
        dk = (jnp.dot(grad_scores, q, preferred_element_type=F32) * score_scale).astype(BF16)
        dq_h = lax.dot_general(
            grad_scores, k, (((0,), (0,)), ((), ())), preferred_element_type=F32
        )
        dq[:, cols] = (dq_h * score_scale).astype(BF16)
        piece = (near.shape[0], near.shape[3], HS)
        for d in range(4):
            part = slice(d * tokens, (d + 1) * tokens)
            z = place[6] if d < 2 else 1 - place[6]
            if d % 2 == 0:
                near[:, z, 0, :, cols] = dk[part].reshape(piece)
                near[:, z, 1, :, cols] = dv[part].reshape(piece)
            else:
                far_keys[:, z, :, cols] = dk[part].reshape(piece)
                far_values[:, z, :, cols] = dv[part].reshape(piece)


def pack_terms(dq, near, core_keys, core_values, out):
    share = near.shape[3]
    dq_sum = dq[0].astype(F32)
    for s in range(1, dq.shape[0]):
        dq_sum = dq_sum + dq[s].astype(F32)
    tokens = dq.shape[1] // GROUPS
    rest = jnp.zeros((out.shape[1] - 2 * share - tokens, out.shape[2]), F32)
    tails = [
        jnp.concatenate([dq_sum[x * tokens : (x + 1) * tokens], rest], axis=0).astype(BF16)
        for x in range(GROUPS)
    ]
    for b in range(near.shape[0]):
        for z in range(2):
            for kind, other in enumerate((core_keys, core_values)):
                total = near[b, z, kind].astype(F32) + other[b, z].astype(F32)
                out[2 * b + z, kind * share : (kind + 1) * share] = total.astype(BF16)
            out[2 * b + z, 2 * share :] = tails[b // 4 * 2 + b % 2]


def unpack_terms(place, terms, grad_queries, grad_keys, grad_values):
    share, tokens = grad_keys.shape[1], grad_queries.shape[1]
    width = terms.shape[2]
    for group in range(GROUPS):
        cols = slice(group * width, (group + 1) * width)
        first = group // 2 * 8 + group % 2 * 2
        sources = [first + 4 * x + z for x in range(2) for z in range(2)]
        for kind, out in enumerate((grad_keys, grad_values)):
            part = slice(kind * share, (kind + 1) * share)
            total = terms[sources[0], part].astype(F32)
            for s in sources[1:]:
                total = total + terms[s, part].astype(F32)
            out[0, :, cols] = total.astype(BF16)
        mine = terms[first + 4 * place[1] + place[6], 2 * share :].astype(F32)
        grad_queries[0, :, cols] = mine[:tokens].astype(BF16)


def on_device(sizes, queries, grad_out, attn_out, lse, keys, values, frame_ids, counts):
    low_y, high_x, low_x, high_z = (lax.axis_index(a) for a in ("yl", "xh", "xl", "zh"))
    low_z, high_y, core = (lax.axis_index(a) for a in ("zl", "yh", "c"))
    tokens_here = queries.shape[1]
    heads = lse.shape[2] // GROUPS
    width = heads * HS
    frame_tokens = keys.shape[1]
    spread = sizes["zh"] * sizes["yh"]
    members = GROUPS * spread
    blocks_q = sizes["yl"] * sizes["xh"] * sizes["xl"]
    share = frame_tokens // blocks_q

    group = low_y * 2 + low_x

    def memory_frame(z, c):
        return ((high_z * 2 + z) * sizes["yh"] + high_y) * 2 + c

    place = jnp.stack(
        [
            group,
            high_x,
            memory_frame(low_z, core),
            memory_frame(low_z, 1 - core),
            memory_frame(1 - low_z, core),
            memory_frame(1 - low_z, 1 - core),
            low_z,
        ]
    ).astype(jnp.int32)

    flip = [(0, 1), (1, 0)]
    kv = jnp.stack(
        [lax.dynamic_slice_in_dim(a[0], group * width, width, 1) for a in (keys, values)]
    )
    kv_z = lax.ppermute(kv, "zl", flip)
    kv_own = call(
        pair_frames,
        "pair_frames",
        jax.ShapeDtypeStruct((2,) + kv.shape, BF16),
        [IN_VMEM] * 2,
        kv,
        kv_z,
        cost=LONG,
    )
    kv_core = lax.ppermute(kv_own, "c", flip)

    packed = call(
        functools.partial(pack_rows, heads=heads),
        "pack_rows",
        jax.ShapeDtypeStruct((members, tokens_here, 2 * width + LANES), BF16),
        [IN_SMEM] + [IN_VMEM] * 4,
        place,
        queries,
        grad_out,
        attn_out,
        lse,
    )
    rows = lax.all_to_all(packed, ("zh", "yh", "yl", "xl"), 0, 0, tiled=True)
    rows = rows.reshape(members * tokens_here, -1)

    part = jax.ShapeDtypeStruct((blocks_q, 2, 2, share, width), BF16)
    half = jax.ShapeDtypeStruct((blocks_q, 2, share, width), BF16)
    dq, near, *far = call(
        functools.partial(attention_grads, heads=heads),
        "attention_grads",
        (jax.ShapeDtypeStruct((rows.shape[0], width), BF16), part, half, half),
        [IN_SMEM] * 2 + [IN_VMEM] * 4,
        place,
        counts,
        frame_ids,
        rows,
        kv_own,
        kv_core,
    )

    dq = lax.all_to_all(
        dq.reshape(spread, GROUPS * tokens_here, width), ("zh", "yh"), 0, 0, tiled=True
    )
    from_core = [lax.ppermute(a, "c", flip) for a in far]
    terms = call(
        pack_terms,
        "pack_terms",
        jax.ShapeDtypeStruct((blocks_q * 2, 2 * share + 2 * tokens_here, width), BF16),
        [IN_VMEM] * 4,
        dq,
        near,
        *from_core,
    )
    terms = lax.all_to_all(terms, ("yl", "xh", "xl", "zl"), 0, 0, tiled=True)
    return call(
        unpack_terms,
        "unpack_terms",
        (
            jax.ShapeDtypeStruct(queries.shape, BF16),
            jax.ShapeDtypeStruct((1, share, keys.shape[2]), BF16),
            jax.ShapeDtypeStruct((1, share, keys.shape[2]), BF16),
        ),
        [IN_SMEM, IN_VMEM],
        place,
        terms,
    )


def solution(mesh):
    query, mem = mesh.shape["query"], mesh.shape["mem"]
    sizes = {"yl": query // 4, "xh": 2, "xl": 2, "zh": mem // 16, "zl": 2, "yh": 4, "c": 2}
    if mem < 16:
        sizes.update(zh=1, yh=mem // 4)
    fine = Mesh(mesh.devices.reshape(tuple(sizes.values())), tuple(sizes))
    q_axes, m_axes = ("yl", "xh", "xl"), ("zh", "zl", "yh", "c")
    rows = P(q_axes, m_axes, None)
    frames = P(m_axes, None, None)
    return jax.shard_map(
        functools.partial(on_device, sizes),
        mesh=fine,
        in_specs=(rows, rows, rows, rows, frames, frames, P(), P()),
        out_specs=(rows, P(m_axes, q_axes, None), P(m_axes, q_axes, None)),
        check_vma=False,
    )
```

```python
import functools
import math

import jax
import jax.numpy as jnp
from jax import lax
from jax.experimental import pallas as pl
from jax.experimental.pallas import tpu as pltpu
from jax.sharding import Mesh, PartitionSpec as P

HS = 128
GROUPS = 4
LANES = 128
MASKED = -1e30
F32, BF16 = jnp.float32, jnp.bfloat16
IN_VMEM = pl.BlockSpec(memory_space=pltpu.VMEM)
IN_SMEM = pl.BlockSpec(memory_space=pltpu.SMEM)
LONG = pl.CostEstimate(flops=10**11, bytes_accessed=10**6, transcendentals=0)


def call(body, name, out_shape, in_specs, *args, cost=None):
    return pl.pallas_call(
        body,
        out_shape=out_shape,
        in_specs=in_specs,
        cost_estimate=cost,
        out_specs=jax.tree.map(lambda _: IN_VMEM, out_shape),
        compiler_params=pltpu.CompilerParams(vmem_limit_bytes=20 * 2**20),
        name=name,
    )(*args)


def pack_rows(place, queries, grad_out, attn_out, lse, out, *, heads):
    width = heads * HS
    tokens = queries.shape[1]
    lane = lax.broadcasted_iota(jnp.int32, (tokens, LANES), 1)
    lse_scaled = lse[0] * HS**0.5
    for group in range(GROUPS):
        extra = jnp.where(lane == 4 * heads + place[0], 1.0, 0.0).astype(F32)
        for h in range(heads):
            head = group * heads + h
            cols = slice(head * HS, (head + 1) * HS)
            product = grad_out[0, :, cols].astype(F32) * attn_out[0, :, cols].astype(F32)
            delta = jnp.sum(product, axis=1, keepdims=True)
            for i, value in enumerate((lse_scaled[:, head : head + 1], delta)):
                high = value.astype(BF16).astype(F32)
                extra = jnp.where(lane == 2 * i * heads + h, high, extra)
                extra = jnp.where(lane == (2 * i + 1) * heads + h, value - high, extra)
        cols = slice(group * width, (group + 1) * width)
        row = jnp.concatenate(
            [queries[0, :, cols], grad_out[0, :, cols], extra.astype(BF16)], axis=1
        )
        for s in range(out.shape[0] // GROUPS):
            out[s * GROUPS + group] = row


def pair_frames(kv_own, kv_z, out):
    out[0] = kv_own[...]
    out[1] = kv_z[...]


def attention_grads(
    place, amounts, ids, rows, kv_own, kv_core, dq, near, far_keys, far_values, *, heads
):
    score_scale = HS ** (-0.5)
    exponent_scale = score_scale * math.log2(math.e)
    width = heads * HS
    blocks = (kv_own.at[0], kv_core.at[0], kv_own.at[1], kv_core.at[1])
    tokens = kv_own.shape[2]

    frame = lax.broadcasted_iota(jnp.int32, ids.shape, 0)
    entry = lax.broadcasted_iota(jnp.int32, ids.shape, 1)
    limit = jnp.zeros(ids.shape, jnp.int32)
    for f in range(ids.shape[0]):
        limit = jnp.where(frame == f, amounts[f], limit)
    listed = entry < limit
    row8 = lax.broadcasted_iota(jnp.int32, (ids.shape[0], LANES), 0)
    lane8 = lax.broadcasted_iota(jnp.int32, (ids.shape[0], LANES), 1)
    slot = (row8 >> 2) * 2 + (row8 & 1)
    spot = (lane8 == 4 * heads + slot) & (((row8 >> 1) & 1) == place[1])
    biases = []
    for d in range(4):
        hit = jnp.where((ids[...] == place[2 + d]) & listed, 1.0, 0.0)
        found = jnp.max(hit, axis=1, keepdims=True)
        bias = jnp.sum(jnp.where(spot, (1.0 - found) * MASKED, 0.0), axis=0, keepdims=True)
        biases.append(bias)
    lane = lax.broadcasted_iota(jnp.int32, (1, LANES), 1)
    extra = rows[:, 2 * width :]

    for h in range(heads):
        cols = slice(h * HS, (h + 1) * HS)
        q = rows[:, cols]
        g = rows[:, width + h * HS : width + (h + 1) * HS]
        k = jnp.concatenate([b[0, :, cols] for b in blocks], axis=0)
        v = jnp.concatenate([b[1, :, cols] for b in blocks], axis=0)
        k_rows = [jnp.where((lane == h) | (lane == heads + h), -1.0, b) for b in biases]
        k_pick = jnp.concatenate(
            [jnp.broadcast_to(r.astype(BF16), (tokens, LANES)) for r in k_rows], axis=0
        )
        v_row = jnp.where((lane == 2 * heads + h) | (lane == 3 * heads + h), -1.0, 0.0)
        v_pick = jnp.broadcast_to(v_row.astype(BF16), k_pick.shape)
        contract = (((1,), (1,)), ((), ()))
        scores = lax.dot_general(
            jnp.concatenate([k, k_pick], axis=1),
            jnp.concatenate([q, extra], axis=1),
            contract,
            preferred_element_type=F32,
        )
        probs = jnp.exp2(scores * exponent_scale)
        grad_probs = lax.dot_general(
            jnp.concatenate([v, v_pick], axis=1),
            jnp.concatenate([g, extra], axis=1),
            contract,
            preferred_element_type=F32,
        )
        grad_scores = (probs * grad_probs).astype(BF16)
        dv = jnp.dot(probs.astype(BF16), g, preferred_element_type=F32).astype(BF16)
        dk = (jnp.dot(grad_scores, q, preferred_element_type=F32) * score_scale).astype(BF16)
        dq_h = lax.dot_general(
            grad_scores, k, (((0,), (0,)), ((), ())), preferred_element_type=F32
        )
        dq[:, cols] = (dq_h * score_scale).astype(BF16)
        piece = (near.shape[0], near.shape[3], HS)
        for d in range(4):
            part = slice(d * tokens, (d + 1) * tokens)
            z = place[6] if d < 2 else 1 - place[6]
            if d % 2 == 0:
                near[:, z, 0, :, cols] = dk[part].reshape(piece)
                near[:, z, 1, :, cols] = dv[part].reshape(piece)
            else:
                far_keys[:, z, :, cols] = dk[part].reshape(piece)
                far_values[:, z, :, cols] = dv[part].reshape(piece)


def pack_terms(dq, near, core_keys, core_values, out):
    share = near.shape[3]
    dq_sum = dq[0].astype(F32)
    for s in range(1, dq.shape[0]):
        dq_sum = dq_sum + dq[s].astype(F32)
    tokens = dq.shape[1] // GROUPS
    rest = jnp.zeros((out.shape[1] - 2 * share - tokens, out.shape[2]), F32)
    tails = [
        jnp.concatenate([dq_sum[x * tokens : (x + 1) * tokens], rest], axis=0).astype(BF16)
        for x in range(GROUPS)
    ]
    for b in range(near.shape[0]):
        for z in range(2):
            for kind, other in enumerate((core_keys, core_values)):
                total = near[b, z, kind].astype(F32) + other[b, z].astype(F32)
                out[z * near.shape[0] + b, kind * share : (kind + 1) * share] = total.astype(BF16)
            out[z * near.shape[0] + b, 2 * share :] = tails[b // 4 * 2 + b % 2]


def unpack_terms(place, terms, grad_queries, grad_keys, grad_values):
    share, tokens = grad_keys.shape[1], grad_queries.shape[1]
    width = terms.shape[2]
    for group in range(GROUPS):
        cols = slice(group * width, (group + 1) * width)
        first = group // 2 * 4 + group % 2
        sources = [first + 2 * x + 8 * z for x in range(2) for z in range(2)]
        for kind, out in enumerate((grad_keys, grad_values)):
            part = slice(kind * share, (kind + 1) * share)
            total = terms[sources[0], part].astype(F32)
            for s in sources[1:]:
                total = total + terms[s, part].astype(F32)
            out[0, :, cols] = total.astype(BF16)
        mine = terms[first + 2 * place[1] + 8 * place[6], 2 * share :].astype(F32)
        grad_queries[0, :, cols] = mine[:tokens].astype(BF16)


def on_device(sizes, queries, grad_out, attn_out, lse, keys, values, frame_ids, counts):
    low_y, high_x, low_x, high_z = (lax.axis_index(a) for a in ("yl", "xh", "xl", "zh"))
    low_z, high_y, core = (lax.axis_index(a) for a in ("zl", "yh", "c"))
    tokens_here = queries.shape[1]
    heads = lse.shape[2] // GROUPS
    width = heads * HS
    frame_tokens = keys.shape[1]
    spread = sizes["zh"] * sizes["yh"]
    members = GROUPS * spread
    blocks_q = sizes["yl"] * sizes["xh"] * sizes["xl"]
    share = frame_tokens // blocks_q

    group = low_y * 2 + low_x

    def memory_frame(z, c):
        return ((high_z * 2 + z) * sizes["yh"] + high_y) * 2 + c

    place = jnp.stack(
        [
            group,
            high_x,
            memory_frame(low_z, core),
            memory_frame(low_z, 1 - core),
            memory_frame(1 - low_z, core),
            memory_frame(1 - low_z, 1 - core),
            low_z,
        ]
    ).astype(jnp.int32)

    flip = [(0, 1), (1, 0)]
    kv = jnp.stack(
        [lax.dynamic_slice_in_dim(a[0], group * width, width, 1) for a in (keys, values)]
    )
    kv_z = lax.ppermute(kv, "zl", flip)
    kv_own = call(
        pair_frames,
        "pair_frames",
        jax.ShapeDtypeStruct((2,) + kv.shape, BF16),
        [IN_VMEM] * 2,
        kv,
        kv_z,
        cost=LONG,
    )
    kv_core = lax.ppermute(kv_own, "c", flip)

    packed = call(
        functools.partial(pack_rows, heads=heads),
        "pack_rows",
        jax.ShapeDtypeStruct((members, tokens_here, 2 * width + LANES), BF16),
        [IN_SMEM] + [IN_VMEM] * 4,
        place,
        queries,
        grad_out,
        attn_out,
        lse,
    )
    rows = lax.all_to_all(packed, ("zh", "yh", "yl", "xl"), 0, 0, tiled=True)
    rows = rows.reshape(members * tokens_here, -1)

    part = jax.ShapeDtypeStruct((blocks_q, 2, 2, share, width), BF16)
    half = jax.ShapeDtypeStruct((blocks_q, 2, share, width), BF16)
    dq, near, *far = call(
        functools.partial(attention_grads, heads=heads),
        "attention_grads",
        (jax.ShapeDtypeStruct((rows.shape[0], width), BF16), part, half, half),
        [IN_SMEM] * 2 + [IN_VMEM] * 4,
        place,
        counts,
        frame_ids,
        rows,
        kv_own,
        kv_core,
    )

    dq = lax.all_to_all(
        dq.reshape(spread, GROUPS * tokens_here, width), ("zh", "yh"), 0, 0, tiled=True
    )
    from_core = [lax.ppermute(a, "c", flip) for a in far]
    terms = call(
        pack_terms,
        "pack_terms",
        jax.ShapeDtypeStruct((blocks_q * 2, 2 * share + 2 * tokens_here, width), BF16),
        [IN_VMEM] * 4,
        dq,
        near,
        *from_core,
    )
    terms = lax.all_to_all(terms, ("zl", "yl", "xh", "xl"), 0, 0, tiled=True)
    return call(
        unpack_terms,
        "unpack_terms",
        (
            jax.ShapeDtypeStruct(queries.shape, BF16),
            jax.ShapeDtypeStruct((1, share, keys.shape[2]), BF16),
            jax.ShapeDtypeStruct((1, share, keys.shape[2]), BF16),
        ),
        [IN_SMEM, IN_VMEM],
        place,
        terms,
    )


def solution(mesh):
    query, mem = mesh.shape["query"], mesh.shape["mem"]
    sizes = {"yl": query // 4, "xh": 2, "xl": 2, "zh": mem // 16, "zl": 2, "yh": 4, "c": 2}
    if mem < 16:
        sizes.update(zh=1, yh=mem // 4)
    fine = Mesh(mesh.devices.reshape(tuple(sizes.values())), tuple(sizes))
    q_axes, m_axes = ("yl", "xh", "xl"), ("zh", "zl", "yh", "c")
    rows = P(q_axes, m_axes, None)
    frames = P(m_axes, None, None)
    return jax.shard_map(
        functools.partial(on_device, sizes),
        mesh=fine,
        in_specs=(rows, rows, rows, rows, frames, frames, P(), P()),
        out_specs=(rows, P(m_axes, q_axes, None), P(m_axes, q_axes, None)),
        check_vma=False,
    )
```
